32 devices in a mesh: tensor: 2 (over y), inner: 4 (over x, core), outer: 4 (over z).
Axes of the slice: x: 2, y: 2, z: 4, core: 2. Of those that a mesh axis runs over, the one named last changes fastest.
Arguments:
- tokens: bfloat16 [512, 78, 768], P(('tensor', 'inner', 'outer')), may hold values from -6 to 6
- counts: int32 [2, 256], P(None, ('inner', 'outer')), may hold values from 20 to 78, as said below
- norm1_gain: float32 [768], replicated, may hold values from 0.5 to 1.5
- norm1_shift: float32 [768], replicated, may hold values from -4 to 4
- qkv_weight: bfloat16 [768, 3, 768], P(None, None, 'tensor'), may hold values from -0.21875 to 0.21875
- qv_bias: float32 [2, 768], P(None, 'tensor'), may hold values from -6 to 6
- out_weight: bfloat16 [768, 768], P('tensor'), may hold values from -0.625 to 0.625
- out_bias: float32 [768], replicated, may hold values from -4 to 4
- norm2_gain: float32 [768], replicated, may hold values from 0.5 to 1.5
- norm2_shift: float32 [768], replicated, may hold values from -4 to 4
- up_weight: bfloat16 [768, 3072], P(None, 'tensor'), may hold values from -0.21875 to 0.21875
- up_bias: float32 [3072], P('tensor'), may hold values from -6 to 6
- down_weight: bfloat16 [3072, 768], P('tensor'), may hold values from -0.15625 to 0.15625
- down_bias: float32 [768], replicated, may hold values from -4 to 4
- cotangent: bfloat16 [512, 78, 768], P(('tensor', 'inner', 'outer')), may hold values from -6 to 6
Outputs:
- mixed_out: bfloat16 [512, 78, 768], P(('tensor', 'inner', 'outer'))
- tokens_grad: float32 [512, 78, 768], P(('tensor', 'inner', 'outer'))
- norm1_gain_grad: float32 [768], P('inner')
- norm1_shift_grad: float32 [768], P('inner')
- qkv_weight_grad: float32 [768, 3, 768], P('inner', None, 'tensor')
- qv_bias_grad: float32 [2, 768], P(None, ('tensor', 'inner'))
- out_weight_grad: float32 [768, 768], P(('tensor', 'inner'))
- out_bias_grad: float32 [768], P('inner')
- norm2_gain_grad: float32 [768], P('inner')
- norm2_shift_grad: float32 [768], P('inner')
- up_weight_grad: float32 [768, 3072], P('inner', 'tensor')
- up_bias_grad: float32 [3072], P(('tensor', 'inner'))
- down_weight_grad: float32 [3072, 768], P(('tensor', 'inner'))
- down_bias_grad: float32 [768], P('inner')
The draws below stay inside these ranges and needn't reach their ends.
Inputs may be any that keep to these rules, and one draw needn't show every extreme that they name: `counts`: visible patches of each image; among each device's 16 images one has all 78.
All inputs are finite; a program needn't handle non-finite values.
Results may differ from the reference program's by a relative error of at most 0.02.
Values may be sent and summed in bfloat16 or wider, within the bound.
A program may use at most 192 MiB of HBM per device.

```python
import jax
import jax.numpy as jnp
from jax import lax

D = 768
HEADS = 12
HEAD_DIM = 64
FF = 3072
SEQ = 78
IMG_DEV = 16
IMAGES = 512
N_TENSOR = 2


def draw_counts(key, part):
    key = jax.random.fold_in(key, 5)
    first_key, pick_key, lowest_key = jax.random.split(key, 3)
    visible = jax.random.randint(first_key, (IMAGES,), 20, SEQ + 1)
    block_count = IMAGES // IMG_DEV
    chosen = jax.random.randint(pick_key, (block_count,), 0, IMG_DEV)
    position = jnp.arange(IMAGES)
    full_rows = position % IMG_DEV == jnp.repeat(chosen, IMG_DEV)
    lowest = jax.random.randint(lowest_key, (), 0, IMAGES)
    visible = jnp.where(full_rows, SEQ, visible)
    visible = jnp.where((position == lowest) & jnp.logical_not(full_rows), 20, visible)
    return visible.astype(jnp.int32).reshape(N_TENSOR, IMAGES // N_TENSOR)


def levels(stream_key, shape, cuts, least, largest):
    def one(dim, blocks):
        steps = jax.random.uniform(jax.random.fold_in(jax.random.fold_in(stream_key, 6), dim), (blocks,), jnp.float32, least / len(cuts), largest / len(cuts))
        return jnp.repeat(jnp.exp(steps), shape[dim] // blocks).reshape((-1,) + (1,) * (len(shape) - dim - 1))

    loudness = one(*cuts[0])
    for cut in cuts[1:]:
        loudness = loudness * one(*cut)
    return loudness


def normal_values(rng, dims, spread, limit, cuts=(), dtype=jnp.bfloat16):
    drawn = spread * jax.random.normal(rng, dims, jnp.float32)
    if cuts:
        drawn = drawn * levels(rng, dims, cuts, -0.22, 0.18)
    return jnp.clip(drawn, -limit, limit).astype(dtype)


def setup_inputs(seed: int = 0) -> dict:
    arg_keys = jax.random.split(jax.random.key(seed), 16)
    tokens = normal_values(arg_keys[0], (IMAGES, SEQ, D), 1.0, 6.0, ((0, 32),))
    counts = draw_counts(jax.random.fold_in(arg_keys[15], 71), 0)
    norm1_gain = jnp.clip(1.0 + 0.1 * jax.random.normal(arg_keys[2], (D,), jnp.float32), 0.5, 1.5)
    norm1_shift = normal_values(arg_keys[3], (D,), 0.3, 4.0, (), jnp.float32)
    qkv_weight = normal_values(arg_keys[4], (D, 3, D), D ** -0.5, 0.21875, ((2, 2),))
    qv_bias = normal_values(arg_keys[5], (2, D), 0.5, 6.0, ((1, 2),), jnp.float32)
    out_weight = normal_values(arg_keys[6], (D, D), (D // 8) ** -0.5, 0.625, ((0, 2),))
    out_bias = normal_values(arg_keys[7], (D,), 0.3, 4.0, (), jnp.float32)
    norm2_gain = jnp.clip(1.0 + 0.1 * jax.random.normal(arg_keys[8], (D,), jnp.float32), 0.5, 1.5)
    norm2_shift = normal_values(arg_keys[9], (D,), 0.3, 4.0, (), jnp.float32)
    up_weight = normal_values(arg_keys[10], (D, FF), D ** -0.5, 0.21875, ((1, 2),))
    up_bias = normal_values(arg_keys[11], (FF,), 0.5, 6.0, ((0, 2),), jnp.float32)
    down_weight = normal_values(arg_keys[12], (FF, D), (FF // 2) ** -0.5, 0.15625, ((0, 2),))
    down_bias = normal_values(arg_keys[13], (D,), 0.3, 4.0, (), jnp.float32)
    cotangent = normal_values(arg_keys[14], (IMAGES, SEQ, D), 1.0, 6.0, ((0, 32),))
    return dict(tokens=tokens, counts=counts, norm1_gain=norm1_gain, norm1_shift=norm1_shift, qkv_weight=qkv_weight, qv_bias=qv_bias, out_weight=out_weight, out_bias=out_bias, norm2_gain=norm2_gain, norm2_shift=norm2_shift, up_weight=up_weight, up_bias=up_bias, down_weight=down_weight, down_bias=down_bias, cotangent=cotangent)


@jax.custom_vjp
def low(v):
    return lax.optimization_barrier(v.astype(jnp.bfloat16)).astype(jnp.float32)

@jax.custom_vjp
def low_back(v):
    return v

def low_keep(v):
    return (low(v), None)

def low_pass(kept, grad):
    return (grad,)

def back_keep(v):
    return (v, None)

def back_low(kept, grad):
    return (low(grad),)
low.defvjp(low_keep, low_pass)
low_back.defvjp(back_keep, back_low)

def both_ways(values):
    return low(low_back(values))

def layer_norm(values, norm_gain, norm_shift):
    row_mean = lax.optimization_barrier(jnp.mean(values, axis=-1, keepdims=True))
    centered = values - row_mean
    variance = lax.optimization_barrier(jnp.mean(centered * centered, axis=-1, keepdims=True))
    return centered * lax.rsqrt(variance + 1e-06) * norm_gain + norm_shift

def block_forward(inputs, counts, params):
    norm1_gain, norm1_shift, qkv_weight, qv_bias, out_weight, out_bias, norm2_gain, norm2_shift, up_weight, up_bias, down_weight, down_bias = params
    highest = lax.Precision.HIGHEST
    image_count = inputs.shape[0]
    head_shape = (image_count, SEQ, HEADS, HEAD_DIM)
    normed1 = low(layer_norm(inputs, norm1_gain, norm1_shift))
    projected = jnp.einsum('bsd,dte->bste', normed1, qkv_weight, precision=highest)
    query_part = both_ways(projected[:, :, 0] + qv_bias[0]).reshape(head_shape)
    key_part = both_ways(projected[:, :, 1]).reshape(head_shape)
    value_part = both_ways(projected[:, :, 2] + qv_bias[1]).reshape(head_shape)
    scores = jnp.einsum('bqhe,bkhe->bhqk', query_part, key_part, precision=highest) * HEAD_DIM ** (-0.5)
    scores = low_back(scores)
    key_live = jnp.arange(SEQ)[None, :] < counts[:, None]
    scores = jnp.where(key_live[:, None, None, :], scores, -1000000000.0)
    row_max = lax.optimization_barrier(jnp.max(scores, axis=-1, keepdims=True))
    exp_scores = jnp.exp(scores - row_max)
    attn_probs = low(exp_scores / lax.optimization_barrier(jnp.sum(exp_scores, axis=-1, keepdims=True)))
    attended = jnp.einsum('bhqk,bkhe->bqhe', attn_probs, value_part, precision=highest)
    attended = both_ways(attended.reshape(image_count, SEQ, D))
    middle = inputs + low_back(jnp.matmul(attended, out_weight, precision=highest)) + out_bias
    normed2 = low(layer_norm(middle, norm2_gain, norm2_shift))
    pre_act = low_back(jnp.matmul(normed2, up_weight, precision=highest) + up_bias)
    activated = low(jax.nn.gelu(pre_act, approximate=False))
    return middle + low_back(jnp.matmul(activated, down_weight, precision=highest)) + down_bias

def reference(tokens, counts, norm1_gain, norm1_shift, qkv_weight, qv_bias, out_weight, out_bias, norm2_gain, norm2_shift, up_weight, up_bias, down_weight, down_bias, cotangent):
    params = tuple((weight.astype(jnp.float32) for weight in (norm1_gain, norm1_shift, qkv_weight, qv_bias, out_weight, out_bias, norm2_gain, norm2_shift, up_weight, up_bias, down_weight, down_bias)))
    step_count = IMAGES // IMG_DEV
    scan_inputs = (tokens.reshape(step_count, IMG_DEV, SEQ, D), counts.reshape(step_count, IMG_DEV), cotangent.reshape(step_count, IMG_DEV, SEQ, D))

    def scan_step(totals, image_block):
        token_part, count_part, cot_part = image_block

        def forward(inputs, *weights):
            return block_forward(inputs, count_part, weights)
        layer_out, pullback = jax.vjp(forward, token_part.astype(jnp.float32), *params)
        row_live = (jnp.arange(SEQ)[None, :] < count_part[:, None]).astype(jnp.float32)
        gradients = pullback(cot_part.astype(jnp.float32) * row_live[:, :, None])
        totals = tuple((first_sum + second_sum for first_sum, second_sum in zip(totals, gradients[1:])))
        return (totals, (layer_out.astype(jnp.bfloat16), gradients[0]))
    zero_sums = tuple((jnp.zeros(weight.shape, jnp.float32) for weight in params))
    totals, (mixed_out, tokens_grad) = lax.scan(scan_step, zero_sums, scan_inputs)
    mixed_out = mixed_out.reshape(IMAGES, SEQ, D)
    tokens_grad = tokens_grad.reshape(IMAGES, SEQ, D)
    return (mixed_out, tokens_grad, totals[0], totals[1], totals[2], totals[3], totals[4], totals[5], totals[6], totals[7], totals[8], totals[9], totals[10], totals[11])
```

```python
import functools

import jax
import jax.numpy as jnp
from jax import lax
from jax.experimental import pallas as pl
from jax.experimental.pallas import tpu as pltpu
from jax.sharding import PartitionSpec as P

F32 = jnp.float32
BF16 = jnp.bfloat16
HEAD_DIM = 64
SLOT = 80
QUAD = 4
BLOCKS = 3


def dot(left, right, dims):
    return lax.dot_general(left, right, (dims, ((), ())), preferred_element_type=F32)


NN = ((1,), (0,))
NT = ((1,), (1,))
TN = ((0,), (0,))


def rows_of(index, size):
    return pl.ds(pl.multiple_of(index * size, size), size)


def norm_stats(values):
    mean = jnp.mean(values, axis=-1, keepdims=True)
    centered = values - mean
    rstd = lax.rsqrt(jnp.mean(centered * centered, axis=-1, keepdims=True) + 1e-6)
    return centered * rstd, rstd


def norm_back(grad, values, gain):
    hat, rstd = norm_stats(values)
    scaled = grad * gain
    first = jnp.mean(scaled, axis=-1, keepdims=True)
    second = jnp.mean(scaled * hat, axis=-1, keepdims=True)
    back = rstd * (scaled - first - hat * second)
    gain_grad = jnp.sum(grad * hat, axis=0, keepdims=True)
    shift_grad = jnp.sum(grad, axis=0, keepdims=True)
    return back, gain_grad, shift_grad


def head_masks():
    head = lax.broadcasted_iota(jnp.int32, (SLOT, 256), 1) // HEAD_DIM
    return [[head == 0, head == 1, head == 2], [head == 1, head == 2, head == 3]]


def stack_heads(values, masks):
    zero = jnp.zeros_like(values)
    return jnp.concatenate([jnp.where(mask, values, zero) for mask in masks], axis=0)


def unstack_heads(values, masks):
    parts = [values[SLOT * i : SLOT * (i + 1)] for i in range(3)]
    return sum(jnp.where(mask, part, 0.0) for mask, part in zip(masks, parts))


def put_heads(ref, rows, start, first, second):
    ref[rows, start : start + 128] = first[:, :128].astype(BF16)
    ref[rows, start + 128 : start + 256] = (first[:, 128:] + second[:, :128]).astype(BF16)
    ref[rows, start + 256 : start + 384] = second[:, 128:].astype(BF16)


def attend(count_of, qkv, half, out, probs, scale, unroll):
    def one_image(image, carry):
        rows = rows_of(image, SLOT)
        live = lax.broadcasted_iota(jnp.int32, (SLOT, 3 * SLOT), 0) < count_of(image)
        parts = []
        for group, masks in enumerate(head_masks()):
            at = 128 * group
            query = qkv[half, rows, at : at + 256]
            key = qkv[half, rows, 384 + at : 384 + at + 256]
            value = qkv[half, rows, 768 + at : 768 + at + 256]
            scores = dot(key, stack_heads(query, masks), NT) * scale
            scores = jnp.where(live, scores, -1e9)
            top = jnp.max(scores, axis=0, keepdims=True)
            powers = jnp.exp(scores - top)
            weights = (powers / jnp.sum(powers, axis=0, keepdims=True)).astype(BF16)
            probs[rows_of((half * 16 + image) * 2 + group, SLOT), :] = weights
            parts.append(unstack_heads(dot(weights, value, TN), masks))
        put_heads(out, rows, half * 384, *parts)
        return carry

    lax.fori_loop(0, 16, one_image, 0, unroll=unroll)


def attend_back(qkv, half, out_grad, probs, scale, unroll):
    def one_image(image, carry):
        rows = rows_of(image, SLOT)
        queries, keys, values = [], [], []
        for group, masks in enumerate(head_masks()):
            at = 128 * group
            query = stack_heads(qkv[half, rows, at : at + 256], masks)
            key = qkv[half, rows, 384 + at : 384 + at + 256]
            value = qkv[half, rows, 768 + at : 768 + at + 256]
            grad = out_grad[rows, half * 384 + at : half * 384 + at + 256]
            grad = stack_heads(grad, masks)
            low = probs[rows_of((half * 16 + image) * 2 + group, SLOT), :]
            weights = low.astype(F32)
            prob_grad = dot(value, grad, NT)
            delta = jnp.sum(prob_grad * weights, axis=0, keepdims=True)
            score_grad = (weights * (prob_grad - delta)).astype(BF16)
            values.append(dot(low, grad, NN))
            keys.append(dot(score_grad, query, NN) * scale)
            queries.append(unstack_heads(dot(score_grad, key, TN), masks) * scale)
        put_heads(qkv.at[half], rows, 0, *queries)
        put_heads(qkv.at[half], rows, 384, *keys)
        put_heads(qkv.at[half], rows, 768, *values)
        return carry

    lax.fori_loop(0, 16, one_image, 0, unroll=unroll)


def layer_kernel(
    counts,
    tokens,
    cotangent,
    gain1,
    shift1,
    out_bias,
    gain2,
    shift2,
    down_bias,
    qkv_bias,
    up_bias,
    wqkv,
    wout,
    wup,
    wdown,
    mixed,
    tokens_grad,
    gqkv,
    gout,
    gup,
    gdown,
    vectors,
    qv_sum,
    up_sum,
    x_rows,
    gm,
    h1,
    qkv,
    att,
    probs,
    mid,
    h2,
    acc_y,
    acc_g,
    act,
    act_grad,
    stage_a,
    stage_b,
    mixed_part,
    grad_part,
    sems,
):
    width = x_rows.shape[1]
    tokens_all = x_rows.shape[0]
    quarter = tokens_all // QUAD
    images = tokens.shape[0]
    slots = tokens.shape[1]
    scale = HEAD_DIM**-0.5
    mine = lax.axis_index("tensor")

    def count_of(image):
        return counts[mine, image]

    pending = []

    def send(src, dst, index):
        copy = pltpu.make_async_copy(src, dst, sems.at[index])
        copy.start()
        pending.append(copy)

    def prepare(group, carry):
        for step in range(QUAD):
            image = group * QUAD + step
            base = pl.multiple_of(image * SLOT, SLOT)
            tail = pl.ds(pl.multiple_of(base + 64, 16), 16)
            x_rows[tail, :] = jnp.zeros((16, width), BF16)
            gm[tail, :] = jnp.zeros((16, width), BF16)
            x_rows[pl.ds(base, slots), :] = tokens[image]
            live = lax.broadcasted_iota(jnp.int32, (slots, width), 0) < count_of(image)
            gy = jnp.where(live, cotangent[image].astype(F32), 0.0)
            gm[pl.ds(base, slots), :] = gy.astype(BF16)
        return carry

    lax.fori_loop(0, images // QUAD, prepare, 0)
    vectors[...] = jnp.zeros_like(vectors)

    def first_norm(group, carry):
        rows = rows_of(group, quarter)
        hat, _ = norm_stats(x_rows[rows, :].astype(F32))
        h1[rows, :] = (hat * gain1[...] + shift1[...]).astype(BF16)
        vectors[5:6, :] += jnp.sum(gm[rows, :].astype(F32), axis=0, keepdims=True)
        return carry

    lax.fori_loop(0, QUAD, first_norm, 0)

    for half in range(2):
        for part in range(3):
            cols = slice(384 * part, 384 * (part + 1))
            found = dot(h1[...], wqkv[half, :, cols], NN)
            if part != 1:
                found = found + qkv_bias[half : half + 1, cols]
            qkv[half, :, cols] = found.astype(BF16)
        attend(count_of, qkv, half, att, probs, scale, 8)

    for part in range(2):
        cols = slice(384 * part, 384 * (part + 1))
        mid[:, cols] = (
            x_rows[:, cols].astype(F32) + dot(att[...], wout[:, cols], NN) + out_bias[:, cols]
        )

    def second_norm(group, carry):
        rows = rows_of(group, quarter)
        hat, _ = norm_stats(mid[rows, :])
        h2[rows, :] = (hat * gain2[...] + shift2[...]).astype(BF16)
        return carry

    lax.fori_loop(0, QUAD, second_norm, 0)

    for half in range(2):
        for block in range(BLOCKS):
            index = half * BLOCKS + block
            bias = up_bias[index : index + 1, :]

            def hidden(group, total, index=index, bias=bias):
                rows = rows_of(group, quarter)
                u = dot(h2[rows, :], wup[index], NN) + bias
                cdf = 0.5 * (1.0 + lax.erf(u * 0.7071067811865476))
                act[rows, :] = (u * cdf).astype(BF16)
                slope = cdf + u * jnp.exp(-0.5 * u * u) * 0.3989422804014327
                low = (dot(gm[rows, :], wdown[index], NT) * slope).astype(BF16)
                act_grad[rows, :] = low
                return total + jnp.sum(low.astype(F32), axis=0, keepdims=True)

            total = lax.fori_loop(0, QUAD, hidden, jnp.zeros((1, 512), F32))
            up_sum[index : index + 1, :] = total
            for part in range(2):
                cols = slice(384 * part, 384 * (part + 1))
                y = dot(act[...], wdown[index, :, cols], NN)
                g = dot(act_grad[...], wup[index, cols, :], NT)
                if index == 0:
                    acc_y[:, cols] = y
                    acc_g[:, cols] = g
                else:
                    acc_y[:, cols] += y
                    acc_g[:, cols] += g
            slot = index % 2
            if index >= 2:
                pending.pop(0).wait()
                pending.pop(0).wait()
            stage_a[slot, 0, :, :512] = dot(h2[...], act_grad[...], TN).astype(BF16)
            send(stage_a.at[slot, 0, :, pl.ds(0, 512)], gup.at[index], 2 * slot)
            stage_a[slot, 1, :, :512] = dot(gm[...], act[...], TN).astype(BF16)
            send(stage_a.at[slot, 1, :, pl.ds(0, 512)], gdown.at[index], 2 * slot + 1)

    def ship(part, whole, group, index):
        slot = lax.rem(group, 2)
        return pltpu.make_async_copy(
            part.at[slot], whole.at[pl.ds(group * QUAD, QUAD)], sems.at[index + slot]
        )

    def before(part, whole, group, index):
        @pl.when(group >= 2)
        def _():
            ship(part, whole, group - 2, index).wait()

    def after(part, whole, index):
        for group in (QUAD - 2, QUAD - 1):
            ship(part, whole, jnp.int32(group), index).wait()

    def finish(group, carry):
        rows = rows_of(group, quarter)
        before(mixed_part, mixed, group, 6)
        values = mid[rows, :]
        y = (values + acc_y[rows, :] + down_bias[...]).astype(BF16)
        for step in range(QUAD):
            mixed_part[lax.rem(group, 2), step] = y[SLOT * step : SLOT * step + slots]
        ship(mixed_part, mixed, group, 6).start()
        back, gain_grad, shift_grad = norm_back(acc_g[rows, :], values, gain2[...])
        grad = gm[rows, :].astype(F32) + back
        acc_g[rows, :] = grad
        gm[rows, :] = grad.astype(BF16)
        vectors[2:3, :] += jnp.sum(grad, axis=0, keepdims=True)
        vectors[3:4, :] += gain_grad
        vectors[4:5, :] += shift_grad
        return carry

    lax.fori_loop(0, QUAD, finish, 0)
    after(mixed_part, mixed, 6)

    out_grad = h2
    for part in range(2):
        cols = slice(384 * part, 384 * (part + 1))
        out_grad[:, cols] = dot(gm[...], wout[cols, :], NT).astype(BF16)
    while pending:
        pending.pop(0).wait()
    stage_a[0, 0] = dot(att[...], gm[...], TN).astype(BF16)
    send(stage_a.at[0, 0], gout, 0)

    for half in range(2):
        attend_back(qkv, half, out_grad, probs, scale, 8)
        for part in range(3):
            cols = slice(384 * part, 384 * (part + 1))
            grads = qkv[half, :, cols]
            stage_b[half, :, cols] = dot(h1[...], grads, TN).astype(BF16)
            if part != 1:
                at = part // 2
                qv_sum[2 * half + at : 2 * half + at + 1, :] = jnp.sum(
                    grads.astype(F32), axis=0, keepdims=True
                )
        send(stage_b.at[half], gqkv.at[half], 4 + half)

    for part in range(2):
        cols = slice(384 * part, 384 * (part + 1))
        acc_y[:, cols] = dot(qkv[0], wqkv[0, cols, :], NT)
        acc_y[:, cols] += dot(qkv[1], wqkv[1, cols, :], NT)

    def last_norm(group, carry):
        rows = rows_of(group, quarter)
        before(grad_part, tokens_grad, group, 8)
        values = x_rows[rows, :].astype(F32)
        back, gain_grad, shift_grad = norm_back(acc_y[rows, :], values, gain1[...])
        grad = acc_g[rows, :] + back
        for step in range(QUAD):
            grad_part[lax.rem(group, 2), step] = grad[SLOT * step : SLOT * step + slots]
        ship(grad_part, tokens_grad, group, 8).start()
        vectors[0:1, :] += gain_grad
        vectors[1:2, :] += shift_grad
        return carry

    lax.fori_loop(0, QUAD, last_norm, 0)
    after(grad_part, tokens_grad, 8)
    while pending:
        pending.pop(0).wait()


def run_layer(counts, tokens, cotangent, rows, qkv_bias, up_bias, wqkv, wout, wup, wdown):
    images, slots, width = tokens.shape
    total = images * SLOT
    half = wqkv.shape[2]
    vmem = pl.BlockSpec(memory_space=pltpu.VMEM)
    anywhere = pl.BlockSpec(memory_space=pl.ANY)
    shape = jax.ShapeDtypeStruct
    return pl.pallas_call(
        layer_kernel,
        out_shape=[
            shape((images, slots, width), BF16),
            shape((images, slots, width), F32),
            shape(wqkv.shape, BF16),
            shape(wout.shape, BF16),
            shape(wup.shape, BF16),
            shape(wup.shape, BF16),
            shape((8, width), F32),
            shape((4, half // 3), F32),
            shape(up_bias.shape, F32),
        ],
        in_specs=[pl.BlockSpec(memory_space=pltpu.SMEM)] + [vmem] * 14,
        out_specs=[anywhere] * 6 + [vmem] * 3,
        scratch_shapes=[
            pltpu.VMEM((total, width), BF16),
            pltpu.VMEM((total, width), BF16),
            pltpu.VMEM((total, width), BF16),
            pltpu.VMEM((2, total, half), BF16),
            pltpu.VMEM((total, width), BF16),
            pltpu.VMEM((4 * images * SLOT, 3 * SLOT), BF16),
            pltpu.VMEM((total, width), F32),
            pltpu.VMEM((total, width), BF16),
            pltpu.VMEM((total, width), F32),
            pltpu.VMEM((total, width), F32),
            pltpu.VMEM((total, 512), BF16),
            pltpu.VMEM((total, 512), BF16),
            pltpu.VMEM((2, 2, width, width), BF16),
            pltpu.VMEM((2, width, half), BF16),
            pltpu.VMEM((2, QUAD, slots, width), BF16),
            pltpu.VMEM((2, QUAD, slots, width), F32),
            pltpu.SemaphoreType.DMA((10,)),
        ],
        compiler_params=pltpu.CompilerParams(vmem_limit_bytes=64 * 2**20 - 2**17),
    )(counts, tokens, cotangent, *rows, qkv_bias, up_bias, wqkv, wout, wup, wdown)


def local(
    tokens,
    counts,
    norm1_gain,
    norm1_shift,
    qkv_weight,
    qv_bias,
    out_weight,
    out_bias,
    norm2_gain,
    norm2_shift,
    up_weight,
    up_bias,
    down_weight,
    down_bias,
    cotangent,
):
    width = tokens.shape[2]
    inner = lax.axis_size("inner")
    head_width = qkv_weight.shape[2]
    hidden = up_weight.shape[1]

    def both(own):
        other = lax.ppermute(own, "tensor", [(0, 1), (1, 0)])
        return jnp.stack([own, other])

    wqkv = both(qkv_weight.reshape(width, 3 * head_width))
    wout = both(out_weight).reshape(2 * head_width, width)
    cut = (4, BLOCKS, 128)
    wup = both(
        up_weight.reshape(width, *cut).transpose(2, 0, 1, 3).reshape(BLOCKS, width, 512)
    ).reshape(2 * BLOCKS, width, 512)
    wdown = both(
        down_weight.reshape(*cut, width).transpose(1, 0, 2, 3).reshape(BLOCKS, 512, width)
    ).reshape(2 * BLOCKS, 512, width)
    up_rows = both(up_bias.reshape(cut).transpose(1, 0, 2).reshape(BLOCKS, 512)).reshape(
        2 * BLOCKS, 512
    )
    zero = jnp.zeros_like(qv_bias[0])
    qkv_rows = both(jnp.concatenate([qv_bias[0], zero, qv_bias[1]]))
    rows = [
        v.reshape(1, width)
        for v in (norm1_gain, norm1_shift, out_bias, norm2_gain, norm2_shift, down_bias)
    ]
    mixed, tokens_grad, gqkv, gout, gup, gdown, vectors, qv_sum, up_sum = run_layer(
        counts, tokens, cotangent, rows, qkv_rows, up_rows, wqkv, wout, wup, wdown
    )

    def own_half(grads):
        other = lax.ppermute(grads[1].astype(BF16), "tensor", [(0, 1), (1, 0)])
        return (grads[0].astype(F32) + other.astype(F32)).astype(BF16)

    gqkv = own_half(gqkv)
    gout = own_half(gout.reshape(2, head_width, width))
    back = lambda v: v.reshape(BLOCKS, width, 4, 128).transpose(1, 2, 0, 3).reshape(width, hidden)
    gup = back(own_half(gup.reshape(2, BLOCKS, width, 512)))
    gdown = back(own_half(gdown.reshape(2, BLOCKS, width, 512))).T
    qv_sum = own_half(qv_sum.reshape(2, 2, head_width))
    up_sum = own_half(up_sum.reshape(2, BLOCKS, 512))
    up_sum = up_sum.reshape(BLOCKS, 4, 128).transpose(1, 0, 2).reshape(hidden)
    vectors = lax.psum(vectors.astype(BF16), "tensor")

    def reduce(grads, dim=0):
        part = lax.psum_scatter(grads, "inner", scatter_dimension=dim, tiled=True)
        return lax.psum(part, "outer").astype(F32)

    gqkv = reduce(gqkv).reshape(width // inner, 3, head_width)
    gout = reduce(gout)
    gup = reduce(gup)
    gdown = reduce(gdown)
    vectors = reduce(vectors.T)
    qv_sum = reduce(qv_sum.T).T
    up_sum = reduce(up_sum)
    return (
        mixed,
        tokens_grad,
        vectors[:, 0],
        vectors[:, 1],
        gqkv,
        qv_sum,
        gout,
        vectors[:, 2],
        vectors[:, 3],
        vectors[:, 4],
        gup,
        up_sum,
        gdown,
        vectors[:, 5],
    )


def solution(mesh):
    in_specs = (
        P(("tensor", "inner", "outer"), None, None),
        P(None, ("inner", "outer")),
        P(),
        P(),
        P(None, None, "tensor"),
        P(None, "tensor"),
        P("tensor", None),
        P(),
        P(),
        P(),
        P(None, "tensor"),
        P("tensor"),
        P("tensor", None),
        P(),
        P(("tensor", "inner", "outer"), None, None),
    )
    out_specs = (
        P(("tensor", "inner", "outer"), None, None),
        P(("tensor", "inner", "outer"), None, None),
        P("inner"),
        P("inner"),
        P("inner", None, "tensor"),
        P(None, ("tensor", "inner")),
        P(("tensor", "inner"), None),
        P("inner"),
        P("inner"),
        P("inner"),
        P("inner", "tensor"),
        P(("tensor", "inner")),
        P(("tensor", "inner"), None),
        P("inner"),
    )
    return jax.shard_map(local, mesh=mesh, in_specs=in_specs, out_specs=out_specs, check_vma=False)
```

```python
import functools

import jax
import jax.numpy as jnp
from jax import lax
from jax.experimental import pallas as pl
from jax.experimental.pallas import tpu as pltpu
from jax.sharding import PartitionSpec as P

F32 = jnp.float32
BF16 = jnp.bfloat16
HEAD_DIM = 64
SLOT = 80
QUAD = 4
MESH = pl.DeviceIdType.MESH
BLOCKS = 3


def dot(left, right, dims):
    return lax.dot_general(left, right, (dims, ((), ())), preferred_element_type=F32)


NN = ((1,), (0,))
NT = ((1,), (1,))
TN = ((0,), (0,))


def rows_of(index, size):
    return pl.ds(pl.multiple_of(index * size, size), size)


def norm_stats(values):
    mean = jnp.mean(values, axis=-1, keepdims=True)
    centered = values - mean
    rstd = lax.rsqrt(jnp.mean(centered * centered, axis=-1, keepdims=True) + 1e-6)
    return centered * rstd, rstd


def norm_back(grad, values, gain):
    hat, rstd = norm_stats(values)
    scaled = grad * gain
    first = jnp.mean(scaled, axis=-1, keepdims=True)
    second = jnp.mean(scaled * hat, axis=-1, keepdims=True)
    back = rstd * (scaled - first - hat * second)
    gain_grad = jnp.sum(grad * hat, axis=0, keepdims=True)
    shift_grad = jnp.sum(grad, axis=0, keepdims=True)
    return back, gain_grad, shift_grad


def head_masks():
    head = lax.broadcasted_iota(jnp.int32, (SLOT, 256), 1) // HEAD_DIM
    return [[head == 0, head == 1, head == 2], [head == 1, head == 2, head == 3]]


def stack_heads(values, masks):
    zero = jnp.zeros_like(values)
    return jnp.concatenate([jnp.where(mask, values, zero) for mask in masks], axis=0)


def unstack_heads(values, masks):
    parts = [values[SLOT * i : SLOT * (i + 1)] for i in range(3)]
    return sum(jnp.where(mask, part, 0.0) for mask, part in zip(masks, parts))


def put_heads(ref, rows, start, first, second):
    ref[rows, start : start + 128] = first[:, :128].astype(BF16)
    ref[rows, start + 128 : start + 256] = (first[:, 128:] + second[:, :128]).astype(BF16)
    ref[rows, start + 256 : start + 384] = second[:, 128:].astype(BF16)


def attend(count_of, qkv, half, out, probs, scale, images):
    def one_image(image, carry):
        rows = rows_of(image, SLOT)
        live = lax.broadcasted_iota(jnp.int32, (SLOT, 3 * SLOT), 0) < count_of(image)
        parts = []
        for group, masks in enumerate(head_masks()):
            at = 128 * group
            query = qkv[half, rows, at : at + 256]
            key = qkv[half, rows, 384 + at : 384 + at + 256]
            value = qkv[half, rows, 768 + at : 768 + at + 256]
            scores = dot(key, stack_heads(query, masks), NT) * scale
            scores = jnp.where(live, scores, -1e9)
            top = jnp.max(scores, axis=0, keepdims=True)
            powers = jnp.exp(scores - top)
            weights = (powers / jnp.sum(powers, axis=0, keepdims=True)).astype(BF16)
            probs[rows_of((half * 16 + image) * 2 + group, SLOT), :] = weights
            parts.append(unstack_heads(dot(weights, value, TN), masks))
        put_heads(out, rows, half * 384, *parts)
        return carry

    lax.fori_loop(*images, one_image, 0, unroll=8)


def attend_back(qkv, half, out_grad, probs, scale, images):
    def one_image(image, carry):
        rows = rows_of(image, SLOT)
        queries, keys, values = [], [], []
        for group, masks in enumerate(head_masks()):
            at = 128 * group
            query = stack_heads(qkv[half, rows, at : at + 256], masks)
            key = qkv[half, rows, 384 + at : 384 + at + 256]
            value = qkv[half, rows, 768 + at : 768 + at + 256]
            grad = out_grad[rows, half * 384 + at : half * 384 + at + 256]
            grad = stack_heads(grad, masks)
            low = probs[rows_of((half * 16 + image) * 2 + group, SLOT), :]
            weights = low.astype(F32)
            prob_grad = dot(value, grad, NT)
            delta = jnp.sum(prob_grad * weights, axis=0, keepdims=True)
            score_grad = (weights * (prob_grad - delta)).astype(BF16)
            values.append(dot(low, grad, NN))
            keys.append(dot(score_grad, query, NN) * scale)
            queries.append(unstack_heads(dot(score_grad, key, TN), masks) * scale)
        put_heads(qkv.at[half], rows, 0, *queries)
        put_heads(qkv.at[half], rows, 384, *keys)
        put_heads(qkv.at[half], rows, 768, *values)
        return carry

    lax.fori_loop(*images, one_image, 0, unroll=8)


class Gather:
    def __init__(self, own, other, place, send, recv):
        self.place, self.send, self.recv = place, send, recv
        tensor, inner, outer = place.at
        whole = not place.split
        self.hop_y = self.copy(own(inner, whole), other(inner, whole), 0, place.over_y)
        self.hops = [self.hop_y]
        if place.split:
            across = lax.rem(inner + 2, 4)
            mine, theirs = other(inner, False), other(across, False)
            self.hop_x = self.copy(mine, mine, 1, place.over_x)
            self.hop_c = self.copy(mine, mine, 2, place.over_core)
            self.hop_xc = self.copy(theirs, theirs, 3, place.over_core)
            self.hops += [self.hop_x, self.hop_c, self.hop_xc]

    def copy(self, src, dst, kind, device):
        return pltpu.make_async_remote_copy(
            src_ref=src,
            dst_ref=dst,
            send_sem=self.send.at[kind],
            recv_sem=self.recv.at[kind],
            device_id=device,
            device_id_type=MESH,
        )

    def first(self):
        self.hop_y.start()

    def second(self):
        self.hop_y.wait_recv()
        if self.place.split:
            self.hop_x.start()
            self.hop_c.start()

    def third(self):
        if self.place.split:
            self.hop_x.wait_recv()
            self.hop_xc.start()

    def ready(self):
        if self.place.split:
            self.hop_c.wait_recv()
            self.hop_xc.wait_recv()

    def sent(self):
        self.hop_y.wait_send()
        self.handed_on()

    def handed_on(self):
        for hop in self.hops[1:]:
            hop.wait_send()


class Place:
    def __init__(self, split):
        self.split = split
        tensor, inner, outer = (lax.axis_index(a) for a in ("tensor", "inner", "outer"))
        self.at = (tensor, inner, outer)
        self.over_y = (1 - tensor, inner, outer)
        if split:
            core = lax.rem(inner, 2)
            self.over_x = (tensor, lax.rem(inner + 2, 4), outer)
            self.over_core = (tensor, inner + 1 - 2 * core, outer)

    def meet(self):
        partners = [self.over_y]
        if self.split:
            partners += [self.over_x, self.over_core]
        barrier = pltpu.get_barrier_semaphore()
        for device in partners:
            pl.semaphore_signal(barrier, inc=1, device_id=device, device_id_type=MESH)
        pl.semaphore_wait(barrier, len(partners))


def row_part(ref, lead, total, count):
    def part(index, whole):
        if whole:
            return ref.at[(*lead, pl.ds(0, total))]
        size = total // count
        return ref.at[(*lead, rows_of(index, size))]

    return part


def layer_kernel(
    split,
    counts,
    tokens,
    cotangent,
    gain1_ref,
    shift1_ref,
    out_bias_ref,
    gain2_ref,
    shift2_ref,
    down_bias_ref,
    qv_bias,
    up_bias,
    qkv_weight,
    out_weight,
    up_weight,
    down_weight,
    mixed,
    tokens_grad,
    gqkv,
    gout,
    gup,
    gdown,
    vectors,
    qv_sum,
    up_sum,
    staged,
    wqkv,
    wout,
    wup,
    wdown,
    biases,
    x_rows,
    gm,
    h1,
    qkv,
    att,
    probs,
    mid,
    h2,
    acc_y,
    acc_g,
    act,
    act_grad,
    mixed_part,
    sems,
    out_sems,
    send,
    recv,
):
    total, width = x_rows.shape
    quarter = total // QUAD
    slots, images = tokens.shape[:2]
    half_width = qkv_weight.shape[2]
    scale = HEAD_DIM**-0.5
    place = Place(split)
    mine = place.at[0]

    def count_of(image):
        return counts[mine, image]

    def line(ref):
        return ref[...].reshape(1, width)

    loads = [
        pltpu.make_async_copy(tokens, staged.at[pl.ds(0, slots)], sems.at[0]),
        pltpu.make_async_copy(qkv_weight, wqkv.at[0], sems.at[1]),
        pltpu.make_async_copy(out_weight, wout.at[0], sems.at[2]),
    ]
    for block in range(BLOCKS):
        for q in range(4):
            at = q * 384 + block * 128
            loads.append(
                pltpu.make_async_copy(
                    up_weight.at[:, pl.ds(at, 128)],
                    wup.at[block, :, pl.ds(q * 128, 128)],
                    sems.at[len(loads)],
                )
            )
            loads.append(
                pltpu.make_async_copy(
                    down_weight.at[pl.ds(at, 128)],
                    wdown.at[block, pl.ds(q * 128, 128)],
                    sems.at[len(loads)],
                )
            )
    for load in loads:
        load.start()
    pieces = []

    def piece(own, other):
        index = len(pieces)
        pieces.append(Gather(own, other, place, send.at[index], recv.at[index]))

    for part in range(3):
        piece(
            row_part(qkv_weight, (part,), width, 4), row_part(wqkv, (1, part), width, 4)
        )
    piece(row_part(out_weight, (), half_width, 4), row_part(wout, (1,), half_width, 4))
    for block in range(BLOCKS):
        piece(row_part(wup, (block,), width, 4), row_part(wup, (BLOCKS + block,), width, 4))
        piece(row_part(wdown, (block,), 512, 4), row_part(wdown, (BLOCKS + block,), 512, 4))
    biases[...] = jnp.zeros_like(biases)
    for block in range(BLOCKS):
        for q in range(4):
            at = q * 384 + block * 128
            found = up_bias[pl.ds(at, 128)].reshape(1, 128)
            biases[0, block : block + 1, q * 128 : (q + 1) * 128] = found
    biases[0, 3:5, :half_width] = qv_bias[...]
    place.meet()
    for gather in pieces[:4]:
        gather.first()
    bias_copy = pltpu.make_async_remote_copy(
        src_ref=biases.at[0],
        dst_ref=biases.at[1],
        send_sem=send.at[10, 0],
        recv_sem=recv.at[10, 0],
        device_id=place.over_y,
        device_id_type=MESH,
    )
    bias_copy.start()

    staged[slots:, :, :] = jnp.zeros((SLOT - slots, images, width), BF16)

    def by_image(target, masked):
        def some_slots(step, carry):
            values = staged[rows_of(step, 16)].astype(F32)
            values = jnp.swapaxes(values, 0, 1)
            for image in range(images):
                rows = pl.ds(pl.multiple_of(image * SLOT + step * 16, 16), 16)
                found = values[image]
                if masked:
                    slot = lax.broadcasted_iota(jnp.int32, (16, width), 0) + step * 16
                    found = jnp.where(slot < count_of(image), found, 0.0)
                target[rows, :] = found.astype(BF16)
            return carry

        lax.fori_loop(0, SLOT // 16, some_slots, 0)

    loads[0].wait()
    by_image(x_rows, False)
    load = pltpu.make_async_copy(cotangent, staged.at[pl.ds(0, slots)], sems.at[0])
    load.start()
    vectors[...] = jnp.zeros_like(vectors)
    gain1, shift1, gain2, shift2 = (
        line(r) for r in (gain1_ref, shift1_ref, gain2_ref, shift2_ref)
    )
    out_bias, down_bias = line(out_bias_ref), line(down_bias_ref)

    def first_norm(group, carry):
        rows = rows_of(group, quarter)
        hat, _ = norm_stats(x_rows[rows, :].astype(F32))
        h1[rows, :] = (hat * gain1 + shift1).astype(BF16)
        return carry

    lax.fori_loop(0, QUAD, first_norm, 0)
    for later in loads[1:]:
        later.wait()
    for gather in pieces[4:]:
        gather.first()
    pieces[0].second()

    def project(half, part):
        found = dot(h1[...], wqkv[half, part], NN)
        if part != 1:
            row = 3 + part // 2
            found = found + biases[half, row : row + 1, :half_width]
        qkv[half, :, 384 * part : 384 * (part + 1)] = found.astype(BF16)

    for part in range(3):
        project(0, part)
    pieces[1].second()
    attend(count_of, qkv, 0, att, probs, scale, (0, 8))
    pieces[2].second()
    pieces[0].third()
    load.wait()
    by_image(gm, True)
    pieces[1].third()
    attend(count_of, qkv, 0, att, probs, scale, (8, 16))
    pieces[3].second()
    pieces[2].third()
    bias_copy.wait()
    for part in range(3):
        pieces[part].ready()
        project(1, part)
    pieces[3].third()
    pieces[4].second()
    attend(count_of, qkv, 1, att, probs, scale, (0, 8))
    pieces[5].second()
    pieces[4].third()
    attend(count_of, qkv, 1, att, probs, scale, (8, 16))
    pieces[3].ready()

    for part in range(2):
        cols = slice(384 * part, 384 * (part + 1))
        weight = wout[:, :, cols].reshape(width, 384)
        mid[:, cols] = (
            x_rows[:, cols].astype(F32) + dot(att[...], weight, NN) + out_bias[:, cols]
        )

    def second_norm(group, carry):
        rows = rows_of(group, quarter)
        hat, _ = norm_stats(mid[rows, :])
        h2[rows, :] = (hat * gain2 + shift2).astype(BF16)
        vectors[5:6, :] += jnp.sum(gm[rows, :].astype(F32), axis=0, keepdims=True)
        return carry

    lax.fori_loop(0, QUAD, second_norm, 0)
    pieces[6].second()
    pieces[5].third()

    hooks = {
        (0, 0): [pieces[7].second, pieces[6].third],
        (0, 1): [pieces[8].second, pieces[7].third],
        (1, 0): [pieces[9].second, pieces[8].third],
        (1, 1): [pieces[9].third],
    }
    for order in range(2 * BLOCKS):
        half, block = order % 2, order // 2
        index = half * BLOCKS + block
        bias = biases[half, block : block + 1, :]
        if half == 1:
            pieces[4 + 2 * block].ready()
            pieces[5 + 2 * block].ready()

        def hidden(group, carry, index=index, bias=bias):
            rows = rows_of(group, quarter)
            u = dot(h2[rows, :], wup[index], NN) + bias
            cdf = 0.5 * (1.0 + lax.erf(u * 0.7071067811865476))
            act[rows, :] = (u * cdf).astype(BF16)
            slope = cdf + u * jnp.exp(-0.5 * u * u) * 0.3989422804014327
            low = (dot(gm[rows, :], wdown[index], NT) * slope).astype(BF16)
            act_grad[rows, :] = low
            return carry + jnp.sum(low.astype(F32), axis=0, keepdims=True)

        up_sum[index : index + 1, :] = lax.fori_loop(
            0, QUAD, hidden, jnp.zeros((1, 512), F32)
        )
        for step in hooks.get((order, 0), ()):
            step()
        for part in range(2):
            cols = slice(384 * part, 384 * (part + 1))
            y = dot(act[...], wdown[index, :, cols], NN)
            g = dot(act_grad[...], wup[index, cols, :], NT)
            if order == 0:
                acc_y[:, cols] = y
                acc_g[:, cols] = g
            else:
                acc_y[:, cols] += y
                acc_g[:, cols] += g
        for step in hooks.get((order, 1), ()):
            step()
        if half == 1:
            pieces[4 + 2 * block].handed_on()
            pieces[5 + 2 * block].handed_on()
        gup_now = dot(h2[...], act_grad[...], TN).astype(BF16)
        gdown_now = dot(act[...], gm[...], TN).astype(BF16)
        if half == 0:
            pieces[4 + 2 * block].hop_y.wait_send()
            pieces[5 + 2 * block].hop_y.wait_send()
        wup[index] = gup_now
        wdown[index] = gdown_now

    copies = [
        pltpu.make_async_copy(wup, gup, out_sems.at[0]),
        pltpu.make_async_copy(wdown, gdown, out_sems.at[1]),
    ]
    for copy in copies:
        copy.start()

    def ship(group):
        slot = lax.rem(group, 2)
        return pltpu.make_async_copy(
            mixed_part.at[slot], mixed.at[rows_of(group, quarter)], out_sems.at[2 + slot]
        )

    def finish(group, carry):
        rows = rows_of(group, quarter)

        @pl.when(group >= 2)
        def _():
            ship(group - 2).wait()

        values = mid[rows, :]
        mixed_part[lax.rem(group, 2)] = (values + acc_y[rows, :] + down_bias).astype(BF16)
        ship(group).start()
        back, gain_grad, shift_grad = norm_back(acc_g[rows, :], values, gain2)
        grad = gm[rows, :].astype(F32) + back
        acc_g[rows, :] = grad
        gm[rows, :] = grad.astype(BF16)
        vectors[2:3, :] += jnp.sum(grad, axis=0, keepdims=True)
        vectors[3:4, :] += gain_grad
        vectors[4:5, :] += shift_grad
        return carry

    lax.fori_loop(0, QUAD, finish, 0)
    for group in (QUAD - 2, QUAD - 1):
        ship(jnp.int32(group)).wait()

    out_grad = h2
    for half in range(2):
        cols = slice(384 * half, 384 * (half + 1))
        out_grad[:, cols] = dot(gm[...], wout[half], NT).astype(BF16)
    pieces[3].sent()
    for half in range(2):
        cols = slice(384 * half, 384 * (half + 1))
        wout[half] = dot(att[:, cols], gm[...], TN).astype(BF16)
    copies.append(pltpu.make_async_copy(wout, gout, out_sems.at[4]))
    copies[-1].start()
    copies[0].wait()

    for half in (1, 0):
        attend_back(qkv, half, out_grad, probs, scale, (0, 16))
        for part in range(3):
            cols = slice(384 * part, 384 * (part + 1))
            grads = qkv[half, :, cols]
            wup[3 * half + part, :, :384] = dot(h1[...], grads, TN).astype(BF16)
            if part != 1:
                at = 2 * half + part // 2
                qv_sum[at : at + 1, :] = jnp.sum(grads.astype(F32), axis=0, keepdims=True)
            index = 5 + 3 * half + part
            copies.append(
                pltpu.make_async_copy(
                    wup.at[3 * half + part, :, pl.ds(0, 384)],
                    gqkv.at[half, part],
                    out_sems.at[index],
                )
            )
            copies[-1].start()

    def last_norm(group, carry):
        rows = rows_of(group, quarter)
        grad = None
        for half in range(2):
            for part in range(3):
                cols = slice(384 * part, 384 * (part + 1))
                term = dot(qkv[half, rows, cols], wqkv[half, part], NT)
                grad = term if grad is None else grad + term
        values = x_rows[rows, :].astype(F32)
        back, gain_grad, shift_grad = norm_back(grad, values, gain1)
        acc_g[rows, :] += back
        vectors[0:1, :] += gain_grad
        vectors[1:2, :] += shift_grad
        return carry

    lax.fori_loop(0, QUAD, last_norm, 0)
    copies.append(pltpu.make_async_copy(acc_g, tokens_grad, out_sems.at[11]))
    copies[-1].start()
    for copy in copies[1:]:
        copy.wait()
    for gather in pieces[:3]:
        gather.sent()


def run_layer(split, *operands):
    tokens, qkv_weight = operands[1], operands[11]
    slots, images, width = tokens.shape
    total = images * SLOT
    half = qkv_weight.shape[2]
    vmem = pl.BlockSpec(memory_space=pltpu.VMEM)
    anywhere = pl.BlockSpec(memory_space=pl.ANY)
    shape = jax.ShapeDtypeStruct
    return pl.pallas_call(
        functools.partial(layer_kernel, split),
        out_shape=[
            shape((total, width), BF16),
            shape((total, width), F32),
            shape((2, 3, width, half), BF16),
            shape((2, half, width), BF16),
            shape((2 * BLOCKS, width, 512), BF16),
            shape((2 * BLOCKS, 512, width), BF16),
            shape((8, width), F32),
            shape((4, half), F32),
            shape((2 * BLOCKS, 512), F32),
        ],
        in_specs=[pl.BlockSpec(memory_space=pltpu.SMEM)]
        + [anywhere] * 2
        + [vmem] * 8
        + [anywhere] * 4,
        out_specs=[anywhere] * 6 + [vmem] * 3,
        scratch_shapes=[
            pltpu.VMEM((SLOT, images, width), BF16),
            pltpu.VMEM((2, 3, width, half), BF16),
            pltpu.VMEM((2, half, width), BF16),
            pltpu.VMEM((2 * BLOCKS, width, 512), BF16),
            pltpu.VMEM((2 * BLOCKS, 512, width), BF16),
            pltpu.VMEM((2, 8, 512), F32),
            pltpu.VMEM((total, width), BF16),
            pltpu.VMEM((total, width), BF16),
            pltpu.VMEM((total, width), BF16),
            pltpu.VMEM((2, total, 3 * half), BF16),
            pltpu.VMEM((total, width), BF16),
            pltpu.VMEM((4 * images * SLOT, 3 * SLOT), BF16),
            pltpu.VMEM((total, width), F32),
            pltpu.VMEM((total, width), BF16),
            pltpu.VMEM((total, width), F32),
            pltpu.VMEM((total, width), F32),
            pltpu.VMEM((total, 512), BF16),
            pltpu.VMEM((total, 512), BF16),
            pltpu.VMEM((2, total // QUAD, width), BF16),
            pltpu.SemaphoreType.DMA((3 + 8 * BLOCKS,)),
            pltpu.SemaphoreType.DMA((12,)),
            pltpu.SemaphoreType.DMA((11, 4)),
            pltpu.SemaphoreType.DMA((11, 4)),
        ],
        compiler_params=pltpu.CompilerParams(
            collective_id=0, has_side_effects=True, vmem_limit_bytes=64 * 2**20 - 2**17
        ),
    )(*operands)


def local(
    tokens,
    counts,
    norm1_gain,
    norm1_shift,
    qkv_weight,
    qv_bias,
    out_weight,
    out_bias,
    norm2_gain,
    norm2_shift,
    up_weight,
    up_bias,
    down_weight,
    down_bias,
    cotangent,
):
    images, slots, width = tokens.shape
    inner = lax.axis_size("inner")
    head_width = qkv_weight.shape[2]
    hidden = up_weight.shape[1]
    mixed, tokens_grad, gqkv, gout, gup, gdown, vectors, qv_sum, up_sum = run_layer(
        inner == 4,
        counts,
        tokens.transpose(1, 0, 2),
        cotangent.transpose(1, 0, 2),
        norm1_gain,
        norm1_shift,
        out_bias,
        norm2_gain,
        norm2_shift,
        down_bias,
        qv_bias,
        up_bias,
        qkv_weight.transpose(1, 0, 2),
        out_weight,
        up_weight,
        down_weight,
    )
    mixed = mixed.reshape(images, SLOT, width)[:, :slots]
    tokens_grad = tokens_grad.reshape(images, SLOT, width)[:, :slots]

    def own_half(grads):
        other = lax.ppermute(grads[1].astype(BF16), "tensor", [(0, 1), (1, 0)])
        return (grads[0].astype(F32) + other.astype(F32)).astype(BF16)

    gqkv = own_half(gqkv).transpose(1, 0, 2)
    gout = own_half(gout)
    back = lambda v: v.reshape(BLOCKS, width, 4, 128).transpose(1, 2, 0, 3).reshape(width, hidden)
    gup = back(own_half(gup.reshape(2, BLOCKS, width, 512)))
    gdown = own_half(gdown.reshape(2, BLOCKS, 512, width))
    gdown = gdown.reshape(BLOCKS, 4, 128, width).transpose(1, 0, 2, 3).reshape(hidden, width)
    qv_sum = own_half(qv_sum.reshape(2, 2, head_width))
    up_sum = own_half(up_sum.reshape(2, BLOCKS, 512))
    up_sum = up_sum.reshape(BLOCKS, 4, 128).transpose(1, 0, 2).reshape(hidden)
    vectors = lax.psum(vectors.astype(BF16), "tensor")

    def reduce(grads, dim=0):
        part = lax.psum_scatter(grads, "inner", scatter_dimension=dim, tiled=True)
        return lax.psum(part, "outer").astype(F32)

    gqkv = reduce(gqkv)
    gout = reduce(gout)
    gup = reduce(gup)
    gdown = reduce(gdown)
    vectors = reduce(vectors.T)
    qv_sum = reduce(qv_sum.T).T
    up_sum = reduce(up_sum)
    return (
        mixed,
        tokens_grad,
        vectors[:, 0],
        vectors[:, 1],
        gqkv,
        qv_sum,
        gout,
        vectors[:, 2],
        vectors[:, 3],
        vectors[:, 4],
        gup,
        up_sum,
        gdown,
        vectors[:, 5],
    )


def solution(mesh):
    in_specs = (
        P(("tensor", "inner", "outer"), None, None),
        P(None, ("inner", "outer")),
        P(),
        P(),
        P(None, None, "tensor"),
        P(None, "tensor"),
        P("tensor", None),
        P(),
        P(),
        P(),
        P(None, "tensor"),
        P("tensor"),
        P("tensor", None),
        P(),
        P(("tensor", "inner", "outer"), None, None),
    )
    out_specs = (
        P(("tensor", "inner", "outer"), None, None),
        P(("tensor", "inner", "outer"), None, None),
        P("inner"),
        P("inner"),
        P("inner", None, "tensor"),
        P(None, ("tensor", "inner")),
        P(("tensor", "inner"), None),
        P("inner"),
        P("inner"),
        P("inner"),
        P("inner", "tensor"),
        P(("tensor", "inner")),
        P(("tensor", "inner"), None),
        P("inner"),
    )
    return jax.shard_map(local, mesh=mesh, in_specs=in_specs, out_specs=out_specs, check_vma=False)
```

```python
import functools

import jax
import jax.numpy as jnp
from jax import lax
from jax.experimental import pallas as pl
from jax.experimental.pallas import tpu as pltpu
from jax.sharding import PartitionSpec as P

F32 = jnp.float32
BF16 = jnp.bfloat16
HEAD_DIM = 64
SLOT = 80
QUAD = 4
MESH = pl.DeviceIdType.MESH
BLOCKS = 3


def dot(left, right, dims):
    return lax.dot_general(left, right, (dims, ((), ())), preferred_element_type=F32)


NN = ((1,), (0,))
NT = ((1,), (1,))
TN = ((0,), (0,))


def rows_of(index, size):
    return pl.ds(pl.multiple_of(index * size, size), size)


def norm_stats(values):
    mean = jnp.mean(values, axis=-1, keepdims=True)
    centered = values - mean
    rstd = lax.rsqrt(jnp.mean(centered * centered, axis=-1, keepdims=True) + 1e-6)
    return centered * rstd, rstd


def norm_back(grad, values, gain):
    hat, rstd = norm_stats(values)
    scaled = grad * gain
    first = jnp.mean(scaled, axis=-1, keepdims=True)
    second = jnp.mean(scaled * hat, axis=-1, keepdims=True)
    back = rstd * (scaled - first - hat * second)
    gain_grad = jnp.sum(grad * hat, axis=0, keepdims=True)
    shift_grad = jnp.sum(grad, axis=0, keepdims=True)
    return back, gain_grad, shift_grad


def head_masks():
    head = lax.broadcasted_iota(jnp.int32, (SLOT, 256), 1) // HEAD_DIM
    return [[head == 0, head == 1, head == 2], [head == 1, head == 2, head == 3]]


def stack_heads(values, masks):
    zero = jnp.zeros_like(values)
    return jnp.concatenate([jnp.where(mask, values, zero) for mask in masks], axis=0)


def unstack_heads(values, masks):
    parts = [values[SLOT * i : SLOT * (i + 1)] for i in range(3)]
    return sum(jnp.where(mask, part, 0.0) for mask, part in zip(masks, parts))


def put_heads(ref, rows, start, first, second):
    ref[rows, start : start + 128] = first[:, :128].astype(BF16)
    ref[rows, start + 128 : start + 256] = (first[:, 128:] + second[:, :128]).astype(BF16)
    ref[rows, start + 256 : start + 384] = second[:, 128:].astype(BF16)


def attend(count_of, qkv, half, out, probs, scale, images):
    def one_image(image, carry):
        rows = rows_of(image, SLOT)
        live = lax.broadcasted_iota(jnp.int32, (SLOT, 3 * SLOT), 0) < count_of(image)
        parts = []
        for group, masks in enumerate(head_masks()):
            at = 128 * group
            query = qkv[half, rows, at : at + 256]
            key = qkv[half, rows, 384 + at : 384 + at + 256]
            value = qkv[half, rows, 768 + at : 768 + at + 256]
            scores = dot(key, stack_heads(query, masks), NT) * scale
            scores = jnp.where(live, scores, -1e9)
            top = jnp.max(scores, axis=0, keepdims=True)
            powers = jnp.exp(scores - top)
            weights = (powers / jnp.sum(powers, axis=0, keepdims=True)).astype(BF16)
            probs[rows_of((half * 16 + image) * 2 + group, SLOT), :] = weights
            parts.append(unstack_heads(dot(weights, value, TN), masks))
        put_heads(out, rows, half * 384, *parts)
        return carry

    lax.fori_loop(*images, one_image, 0, unroll=8)


def attend_back(qkv, half, out_grad, probs, scale, images):
    def one_image(image, carry):
        rows = rows_of(image, SLOT)
        queries, keys, values = [], [], []
        for group, masks in enumerate(head_masks()):
            at = 128 * group
            query = stack_heads(qkv[half, rows, at : at + 256], masks)
            key = qkv[half, rows, 384 + at : 384 + at + 256]
            value = qkv[half, rows, 768 + at : 768 + at + 256]
            grad = out_grad[rows, half * 384 + at : half * 384 + at + 256]
            grad = stack_heads(grad, masks)
            low = probs[rows_of((half * 16 + image) * 2 + group, SLOT), :]
            weights = low.astype(F32)
            prob_grad = dot(value, grad, NT)
            delta = jnp.sum(prob_grad * weights, axis=0, keepdims=True)
            score_grad = (weights * (prob_grad - delta)).astype(BF16)
            values.append(dot(low, grad, NN))
            keys.append(dot(score_grad, query, NN) * scale)
            queries.append(unstack_heads(dot(score_grad, key, TN), masks) * scale)
        put_heads(qkv.at[half], rows, 0, *queries)
        put_heads(qkv.at[half], rows, 384, *keys)
        put_heads(qkv.at[half], rows, 768, *values)
        return carry

    lax.fori_loop(*images, one_image, 0, unroll=8)


class Gather:
    def __init__(self, own, other, place, send, recv):
        self.place, self.send, self.recv = place, send, recv
        tensor, inner, outer = place.at
        whole = not place.split
        self.hop_y = self.copy(own(inner, whole), other(inner, whole), 0, place.over_y)
        self.hops = [self.hop_y]
        if place.split:
            across = lax.rem(inner + 2, 4)
            mine, theirs = other(inner, False), other(across, False)
            self.hop_x = self.copy(mine, mine, 1, place.over_x)
            self.hop_c = self.copy(mine, mine, 2, place.over_core)
            self.hop_xc = self.copy(theirs, theirs, 3, place.over_core)
            self.hops += [self.hop_x, self.hop_c, self.hop_xc]

    def copy(self, src, dst, kind, device):
        return pltpu.make_async_remote_copy(
            src_ref=src,
            dst_ref=dst,
            send_sem=self.send.at[kind],
            recv_sem=self.recv.at[kind],
            device_id=device,
            device_id_type=MESH,
        )

    def first(self):
        self.hop_y.start()

    def second(self):
        self.hop_y.wait_recv()
        if self.place.split:
            self.hop_x.start()
            self.hop_c.start()

    def third(self):
        if self.place.split:
            self.hop_x.wait_recv()
            self.hop_xc.start()

    def ready(self):
        if self.place.split:
            self.hop_c.wait_recv()
            self.hop_xc.wait_recv()

    def sent(self):
        self.hop_y.wait_send()
        self.handed_on()

    def handed_on(self):
        for hop in self.hops[1:]:
            hop.wait_send()


class Place:
    def __init__(self, split):
        self.split = split
        tensor, inner, outer = (lax.axis_index(a) for a in ("tensor", "inner", "outer"))
        self.at = (tensor, inner, outer)
        self.over_y = (1 - tensor, inner, outer)
        if split:
            core = lax.rem(inner, 2)
            self.over_x = (tensor, lax.rem(inner + 2, 4), outer)
            self.over_core = (tensor, inner + 1 - 2 * core, outer)
            self.over_z = [(tensor, inner, lax.rem(outer + step, 4)) for step in range(1, 4)]

    def meet(self):
        partners = [self.over_y]
        if self.split:
            partners += [self.over_x, self.over_core] + self.over_z
        barrier = pltpu.get_barrier_semaphore()
        for device in partners:
            pl.semaphore_signal(barrier, inc=1, device_id=device, device_id_type=MESH)
        pl.semaphore_wait(barrier, len(partners))


def add_into(target, found):
    target[...] = (target[...].astype(F32) + found[...].astype(F32)).astype(target.dtype)


class Reduce:
    CORE, X, Y, RS, AG = 0, 4, 6, 8, 11

    def __init__(self, grads, size, place, send, recv, core, first, second, outer, x_first):
        self.grads, self.size, self.place = grads, size, place
        self.send, self.recv = send, recv
        self.core, self.first, self.second, self.outer = core, first, second, outer
        self.x_first = x_first
        _, inner, self.z = place.at
        self.c, self.x = lax.rem(inner, 2), inner // 2
        self.inner = inner

    def copy(self, src, dst, kind, device):
        return pltpu.make_async_remote_copy(
            src_ref=src,
            dst_ref=dst,
            send_sem=self.send.at[kind],
            recv_sem=self.recv.at[kind],
            device_id=device,
            device_id_type=MESH,
        )

    def kept(self, half, across):
        return self.grads(half, 2 * across + self.c)

    def core_copies(self, half):
        return [
            self.copy(
                self.grads(half, 2 * across + 1 - self.c),
                self.core(half, across),
                self.CORE + 2 * half + across,
                self.place.over_core,
            )
            for across in range(2)
        ]

    def core_send(self, halves=(0, 1)):
        for half in halves:
            for copy in self.core_copies(half):
                copy.start()

    def core_add(self, halves=(0, 1)):
        for half in halves:
            for across, copy in enumerate(self.core_copies(half)):
                copy.wait()
                add_into(self.kept(half, across), self.core(half, across))

    def x_copy(self, half):
        target = self.first(half) if self.x_first else self.second()
        source = self.kept(half, 1 - self.x)
        return self.copy(source, target, self.X + half, self.place.over_x)

    def x_send(self, halves=None):
        for half in halves or ((0, 1) if self.x_first else (0,)):
            self.x_copy(half).start()

    def x_add(self, halves=None):
        for half in halves or ((0, 1) if self.x_first else (0,)):
            self.x_copy(half).wait()
            add_into(self.kept(half, self.x), self.first(half) if self.x_first else self.second())

    def y_copies(self):
        if self.x_first:
            sent = [(self.kept(1, self.x), self.second())]
        else:
            sent = [(self.kept(1, across), self.first(across)) for across in range(2)]
        return [
            self.copy(src, dst, self.Y + k, self.place.over_y) for k, (src, dst) in enumerate(sent)
        ]

    def y_send(self):
        for copy in self.y_copies():
            copy.start()

    def y_add(self):
        for across, copy in enumerate(self.y_copies()):
            copy.wait()
            if self.x_first:
                add_into(self.kept(0, self.x), self.second())
            else:
                add_into(self.kept(0, across), self.first(across))

    def mine(self):
        return self.grads(0, self.inner)

    def fourth(self, which):
        size = self.size // 4
        return self.grads(0, self.inner, pl.multiple_of(which * size, 16), size)

    def rs_copies(self):
        found = []
        for step in range(1, 4):
            there = lax.rem(self.z + step, 4)
            device = (self.place.at[0], self.inner, there)
            found.append(
                self.copy(self.fourth(there), self.outer(step - 1), self.RS + step - 1, device)
            )
        return found

    def rs_send(self):
        for copy in self.rs_copies():
            copy.start()

    def rs_add(self):
        for copy in self.rs_copies():
            copy.wait()
        total = self.fourth(self.z)[...].astype(F32)
        for step in range(3):
            total = total + self.outer(step)[...].astype(F32)
        self.fourth(self.z)[...] = total.astype(BF16)

    def ag_copies(self):
        found = []
        for step in range(1, 4):
            device = (self.place.at[0], self.inner, lax.rem(self.z + step, 4))
            part = self.fourth(self.z)
            found.append(self.copy(part, self.outer(2 + step), self.AG + step - 1, device))
        return found

    def ag_send(self):
        for copy in self.ag_copies():
            copy.start()

    def ag_wait(self):
        for copy in self.ag_copies():
            copy.wait()

    def summed(self):
        size = self.size // 4
        found = [(self.fourth(self.z), self.z * size)]
        for step in range(1, 4):
            found.append((self.outer(2 + step), lax.rem(self.z + 4 - step, 4) * size))
        return [(ref, pl.ds(pl.multiple_of(row, 16), size)) for ref, row in found]

    def whole_copies(self):
        found = []
        for step in range(1, 4):
            device = (self.place.at[0], self.inner, lax.rem(self.z + step, 4))
            found.append(self.copy(self.mine(), self.outer(step - 1), self.RS + step - 1, device))
        return found

    def whole_send(self):
        for copy in self.whole_copies():
            copy.start()

    def whole_add(self):
        for copy in self.whole_copies():
            copy.wait()
        total = self.mine()[...].astype(F32)
        for step in range(3):
            total = total + self.outer(step)[...].astype(F32)
        self.mine()[...] = total.astype(BF16)


def row_part(ref, lead, total, count):
    def part(index, whole):
        if whole:
            return ref.at[(*lead, pl.ds(0, total))]
        size = total // count
        return ref.at[(*lead, rows_of(index, size))]

    return part


def layer_kernel(
    split,
    counts,
    tokens,
    cotangent,
    gain1_ref,
    shift1_ref,
    out_bias_ref,
    gain2_ref,
    shift2_ref,
    down_bias_ref,
    qv_bias,
    up_bias,
    qkv_weight,
    out_weight,
    up_weight,
    down_weight,
    mixed,
    tokens_grad,
    gqkv,
    gout,
    gup,
    gdown,
    sums,
    staged,
    wqkv,
    wout,
    wup,
    wdown,
    biases,
    x_rows,
    gm,
    h1,
    qkv,
    att,
    probs,
    mid,
    h2,
    acc_y,
    acc_g,
    act,
    act_grad,
    mixed_part,
    sems,
    out_sems,
    send,
    recv,
    core_up,
    core_down,
    first_up,
    first_down,
    second_up,
    second_down,
    outer_up,
    outer_down,
    out_parts,
    sums_in,
    sum_send,
    sum_recv,
    small_send,
    small_recv,
    credit,
):
    total, width = x_rows.shape
    quarter = total // QUAD
    images = counts.shape[1]
    slots = tokens.shape[0] // images
    half_width = qkv_weight.shape[2]
    scale = HEAD_DIM**-0.5
    place = Place(split)
    mine = place.at[0]

    def count_of(image):
        return counts[mine, image]

    def line(ref):
        return ref[...].reshape(1, width)

    loads = [
        pltpu.make_async_copy(tokens, staged.at[pl.ds(0, slots * images)], sems.at[0]),
        pltpu.make_async_copy(qkv_weight, wqkv.at[0], sems.at[1]),
        pltpu.make_async_copy(out_weight, wout.at[0], sems.at[2]),
    ]
    for block in range(BLOCKS):
        for q in range(4):
            at = q * 384 + block * 128
            loads.append(
                pltpu.make_async_copy(
                    up_weight.at[:, pl.ds(at, 128)],
                    wup.at[block, :, pl.ds(q * 128, 128)],
                    sems.at[len(loads)],
                )
            )
            loads.append(
                pltpu.make_async_copy(
                    down_weight.at[pl.ds(at, 128)],
                    wdown.at[block, pl.ds(q * 128, 128)],
                    sems.at[len(loads)],
                )
            )
    for load in loads:
        load.start()
    pieces = []

    def piece(own, other):
        index = len(pieces)
        pieces.append(Gather(own, other, place, send.at[index], recv.at[index]))

    for part in range(3):
        piece(
            row_part(qkv_weight, (part,), width, 4), row_part(wqkv, (1, part), width, 4)
        )
    piece(row_part(out_weight, (), half_width, 4), row_part(wout, (1,), half_width, 4))
    for block in range(BLOCKS):
        piece(row_part(wup, (block,), width, 4), row_part(wup, (BLOCKS + block,), width, 4))
        piece(row_part(wdown, (block,), 512, 4), row_part(wdown, (BLOCKS + block,), 512, 4))
    biases[...] = jnp.zeros_like(biases)
    for block in range(BLOCKS):
        for q in range(4):
            at = q * 384 + block * 128
            found = up_bias[pl.ds(at, 128)].reshape(1, 128)
            biases[0, block : block + 1, q * 128 : (q + 1) * 128] = found
    biases[0, 3:5, :half_width] = qv_bias[...]
    place.meet()
    for gather in pieces[:4]:
        gather.first()
    bias_copy = pltpu.make_async_remote_copy(
        src_ref=biases.at[0],
        dst_ref=biases.at[1],
        send_sem=send.at[10, 0],
        recv_sem=recv.at[10, 0],
        device_id=place.over_y,
        device_id_type=MESH,
    )
    bias_copy.start()

    staged[slots * images :, :] = jnp.zeros(((SLOT - slots) * images, width), BF16)

    def by_image(target, masked):
        def some_slots(step, carry):
            values = staged[rows_of(step, 16 * images), :].astype(F32)
            values = values.reshape(16, images, width)
            values = jnp.swapaxes(values, 0, 1)
            for image in range(images):
                rows = pl.ds(pl.multiple_of(image * SLOT + step * 16, 16), 16)
                found = values[image]
                if masked:
                    slot = lax.broadcasted_iota(jnp.int32, (16, width), 0) + step * 16
                    found = jnp.where(slot < count_of(image), found, 0.0)
                target[rows, :] = found.astype(BF16)
            return carry

        lax.fori_loop(0, SLOT // 16, some_slots, 0)

    loads[0].wait()
    by_image(x_rows, False)
    load = pltpu.make_async_copy(cotangent, staged.at[pl.ds(0, slots * images)], sems.at[0])
    load.start()
    sums[...] = jnp.zeros_like(sums)
    gain1, shift1, gain2, shift2 = (
        line(r) for r in (gain1_ref, shift1_ref, gain2_ref, shift2_ref)
    )
    out_bias, down_bias = line(out_bias_ref), line(down_bias_ref)

    def first_norm(group, carry):
        rows = rows_of(group, quarter)
        hat, _ = norm_stats(x_rows[rows, :].astype(F32))
        h1[rows, :] = (hat * gain1 + shift1).astype(BF16)
        return carry

    lax.fori_loop(0, QUAD, first_norm, 0)
    for later in loads[1:]:
        later.wait()
    for gather in pieces[4:]:
        gather.first()
    pieces[0].second()

    def project(half, part):
        found = dot(h1[...], wqkv[half, part], NN)
        if part != 1:
            row = 3 + part // 2
            found = found + biases[half, row : row + 1, :half_width]
        qkv[half, :, 384 * part : 384 * (part + 1)] = found.astype(BF16)

    for part in range(3):
        project(0, part)
    pieces[1].second()
    attend(count_of, qkv, 0, att, probs, scale, (0, 8))
    pieces[2].second()
    pieces[0].third()
    load.wait()
    by_image(gm, True)
    pieces[1].third()
    attend(count_of, qkv, 0, att, probs, scale, (8, 16))
    pieces[3].second()
    pieces[2].third()
    bias_copy.wait()
    for part in range(3):
        pieces[part].ready()
        project(1, part)
    pieces[3].third()
    pieces[4].second()
    attend(count_of, qkv, 1, att, probs, scale, (0, 8))
    pieces[5].second()
    pieces[4].third()
    attend(count_of, qkv, 1, att, probs, scale, (8, 16))
    pieces[3].ready()

    for part in range(2):
        cols = slice(384 * part, 384 * (part + 1))
        weight = wout[:, :, cols].reshape(width, 384)
        mid[:, cols] = (
            x_rows[:, cols].astype(F32) + dot(att[...], weight, NN) + out_bias[:, cols]
        )

    def second_norm(group, carry):
        rows = rows_of(group, quarter)
        hat, _ = norm_stats(mid[rows, :])
        h2[rows, :] = (hat * gain2 + shift2).astype(BF16)
        sums[1, 5:6, :] += jnp.sum(gm[rows, :].astype(F32), axis=0, keepdims=True)
        return carry

    lax.fori_loop(0, QUAD, second_norm, 0)
    pieces[6].second()
    pieces[5].third()

    inner = place.at[1]

    def up_part(block):
        def part(half, q, start=0, size=192):
            return wup.at[half * BLOCKS + block, pl.ds(pl.multiple_of(q * 192 + start, 16), size)]

        return part

    def down_part(block):
        def part(half, q, start=0, size=128):
            return wdown.at[half * BLOCKS + block, pl.ds(pl.multiple_of(q * 128 + start, 16), size)]

        return part

    def out_part(half, q, start=0, size=96):
        return wout.at[half, pl.ds(pl.multiple_of(q * 96 + start, 16), size)]

    homes = [
        [(gm, 0), (gm, 384), (staged, 384)],
        [(att, 0), (att, 384), (staged, 0)],
    ]

    def qkv_part(which):
        def part(half, q, start=0, size=192):
            ref, col = homes[half][which]
            rows = pl.ds(pl.multiple_of(q * 192 + start, 16), size)
            return ref.at[rows, pl.ds(col, 384)]

        return part

    spare = [
        (ref, row, col) for ref in (att, gm, staged) for row in (768, 960) for col in (0, 384)
    ] + [(ref, 192 * k, 0) for ref in (act, act_grad) for k in range(6)]

    def taken(index):
        ref, row, col = spare[index]
        return ref.at[pl.ds(row, 192), pl.ds(col, 384)]

    few = [
        (ref, row, col) for ref in (att, gm, staged) for row in (1152, 1200) for col in (0, 384)
    ] + [(ref, row, 0) for ref in (act, act_grad) for row in (1152, 1200)]

    def taken_few(part, step):
        if part == 2:
            ref, row, col = act_grad, 576 + 48 * step, 0
        else:
            ref, row, col = few[6 * part + step]
        return ref.at[pl.ds(row, 48), pl.ds(col, 384)]

    ups, downs, qkvs = [], [], []
    if split:
        for block in range(BLOCKS):
            ups.append(
                Reduce(
                    up_part(block), 192, place, sum_send.at[0], sum_recv.at[0],
                    lambda half, across: core_up.at[half, across],
                    lambda across: first_up.at[across],
                    lambda: second_up,
                    lambda step: outer_up.at[step],
                    False,
                )
            )
            downs.append(
                Reduce(
                    down_part(block), 128, place, sum_send.at[1], sum_recv.at[1],
                    lambda half, across: core_down.at[half, across],
                    lambda half: first_down.at[half],
                    lambda: second_down,
                    lambda step: outer_down.at[step],
                    True,
                )
            )
        outs = Reduce(
            out_part, 96, place, sum_send.at[2], sum_recv.at[2],
            lambda half, across: out_parts.at[2 * half + across],
            lambda across: out_parts.at[4 + across],
            lambda: out_parts.at[6],
            lambda step: out_parts.at[7 + step],
            False,
        )
        for part in range(3):
            qkvs.append(
                Reduce(
                    qkv_part(part), 192, place, sum_send.at[3 + part], sum_recv.at[3 + part],
                    lambda half, across, part=part: taken(4 * part + 2 * half + across),
                    lambda half, part=part: taken(12 + 2 * part + half),
                    lambda part=part: taken(18 + part),
                    lambda step, part=part: taken_few(part, step),
                    True,
                )
            )

    def free(index, device):
        pl.semaphore_signal(credit.at[index], inc=1, device_id=device, device_id_type=MESH)

    def may(index, count=1):
        pl.semaphore_wait(credit.at[index], count)

    stores = []

    def store(src, dst):
        copy = pltpu.make_async_copy(src, dst, out_sems.at[12 + len(stores)])
        copy.start()
        stores.append(copy)

    def store_sum(grads, ref, lead):
        for part, rows in grads.summed():
            store(part, ref.at[lead, rows])

    stored = []

    def stored_all():
        for copy in stores[len(stored) :]:
            copy.wait()
            stored.append(copy)

    def step0(block):
        if block:
            may(0)
        ups[block].core_send()
        downs[block].core_send()

    def step1(block):
        ups[block].core_add()
        downs[block].core_add()
        if block < BLOCKS - 1:
            free(0, place.over_core)
        if block:
            may(1)
            may(2)
        ups[block].y_send()
        downs[block].x_send()

    def step2(block):
        ups[block].y_add()
        downs[block].x_add()
        if block < BLOCKS - 1:
            free(1, place.over_y)
            free(2, place.over_x)
        if block:
            may(3)
            may(4)
        ups[block].x_send()
        downs[block].y_send()

    def step3(block):
        ups[block].x_add()
        downs[block].y_add()
        if block < BLOCKS - 1:
            free(3, place.over_x)
            free(4, place.over_y)
        stored_all()
        ups[block].rs_send()
        downs[block].rs_send()

    def step4(block):
        ups[block].rs_add()
        downs[block].rs_add()
        ups[block].ag_send()
        downs[block].ag_send()

    def step5(block):
        ups[block].ag_wait()
        downs[block].ag_wait()
        store_sum(ups[block], gup, block)
        store_sum(downs[block], gdown, block)

    hooks = {
        (0, 0): [pieces[7].second, pieces[6].third],
        (0, 1): [pieces[8].second, pieces[7].third],
        (1, 0): [pieces[9].second, pieces[8].third],
        (1, 1): [pieces[9].third],
    }
    if split:
        hooks.update(
            {
                (1, 2): [lambda: step0(0)],
                (2, 0): [lambda: step1(0)],
                (3, 0): [lambda: step2(0)],
                (3, 2): [lambda: step0(1)],
                (4, 0): [lambda: step3(0), lambda: step1(1)],
                (5, 0): [lambda: step4(0), lambda: step2(1)],
                (5, 2): [lambda: step0(2)],
            }
        )
    for order in range(2 * BLOCKS):
        half, block = order % 2, order // 2
        index = half * BLOCKS + block
        bias = biases[half, block : block + 1, :]
        if half == 1:
            pieces[4 + 2 * block].ready()
            pieces[5 + 2 * block].ready()

        def hidden(group, carry, index=index, bias=bias):
            rows = rows_of(group, quarter)
            u = dot(h2[rows, :], wup[index], NN) + bias
            cdf = 0.5 * (1.0 + lax.erf(u * 0.7071067811865476))
            act[rows, :] = (u * cdf).astype(BF16)
            slope = cdf + u * jnp.exp(-0.5 * u * u) * 0.3989422804014327
            low = (dot(gm[rows, :], wdown[index], NT) * slope).astype(BF16)
            act_grad[rows, :] = low
            return carry + jnp.sum(low.astype(F32), axis=0, keepdims=True)

        sums[2 * half, 2 + block : 3 + block, :512] = lax.fori_loop(
            0, QUAD, hidden, jnp.zeros((1, 512), F32)
        )
        for step in hooks.get((order, 0), ()):
            step()
        for part in range(2):
            cols = slice(384 * part, 384 * (part + 1))
            y = dot(act[...], wdown[index, :, cols], NN)
            g = dot(act_grad[...], wup[index, cols, :], NT)
            if order == 0:
                acc_y[:, cols] = y
                acc_g[:, cols] = g
            else:
                acc_y[:, cols] += y
                acc_g[:, cols] += g
        for step in hooks.get((order, 1), ()):
            step()
        if half == 1:
            pieces[4 + 2 * block].handed_on()
            pieces[5 + 2 * block].handed_on()
        gup_now = dot(h2[...], act_grad[...], TN).astype(BF16)
        gdown_now = dot(act[...], gm[...], TN).astype(BF16)
        if half == 0:
            pieces[4 + 2 * block].hop_y.wait_send()
            pieces[5 + 2 * block].hop_y.wait_send()
        wup[index] = gup_now
        wdown[index] = gdown_now
        for step in hooks.get((order, 2), ()):
            step()

    if not split:
        store(wup, gup)
        store(wdown, gdown)

    def ship(group):
        slot = lax.rem(group, 2)
        return pltpu.make_async_copy(
            mixed_part.at[slot], mixed.at[rows_of(group, quarter)], out_sems.at[2 + slot]
        )

    def finish(group, carry):
        rows = rows_of(group, quarter)

        @pl.when(group >= 2)
        def _():
            ship(group - 2).wait()

        values = mid[rows, :]
        mixed_part[lax.rem(group, 2)] = (values + acc_y[rows, :] + down_bias).astype(BF16)
        ship(group).start()
        back, gain_grad, shift_grad = norm_back(acc_g[rows, :], values, gain2)
        grad = gm[rows, :].astype(F32) + back
        acc_g[rows, :] = grad
        gm[rows, :] = grad.astype(BF16)
        sums[1, 2:3, :] += jnp.sum(grad, axis=0, keepdims=True)
        sums[1, 3:4, :] += gain_grad
        sums[1, 4:5, :] += shift_grad
        return carry

    lax.fori_loop(0, QUAD, finish, 0)
    for group in (QUAD - 2, QUAD - 1):
        ship(jnp.int32(group)).wait()
    if split:
        step5(0)
        step3(1)
        step1(2)

    out_grad = h2
    for half in range(2):
        cols = slice(384 * half, 384 * (half + 1))
        out_grad[:, cols] = dot(gm[...], wout[half], NT).astype(BF16)
    pieces[3].sent()
    for half in range(2):
        cols = slice(384 * half, 384 * (half + 1))
        wout[half] = dot(att[:, cols], gm[...], TN).astype(BF16)
    if split:
        outs.core_send()
        free(5, place.over_core)
        free(6, place.over_x)
        free(7, place.over_y)
        for device in place.over_z:
            free(8, device)
    else:
        store(wout, gout)

    def qkv_grads(half):
        for part in range(3):
            cols = slice(384 * part, 384 * (part + 1))
            grads = qkv[half, :, cols]
            home, col = homes[half][part]
            home[:width, col : col + 384] = dot(h1[...], grads, TN).astype(BF16)
            if part != 1:
                at = part // 2
                sums[2 * half, at : at + 1, :half_width] = jnp.sum(
                    grads.astype(F32), axis=0, keepdims=True
                )
            if not split:
                store(home.at[pl.ds(0, width), pl.ds(col, 384)], gqkv.at[half, part])

    attend_back(qkv, 1, out_grad, probs, scale, (0, 8))
    if split:
        outs.core_add()
        outs.y_send()
        step4(1)
        step2(2)
    attend_back(qkv, 1, out_grad, probs, scale, (8, 16))
    qkv_grads(1)
    if split:
        may(5)
        for grads in qkvs:
            grads.core_send((1,))
        outs.y_add()
        outs.x_send()
        step5(1)
        step3(2)
    attend_back(qkv, 0, out_grad, probs, scale, (0, 8))
    if split:
        may(6)
        for grads in qkvs:
            grads.core_add((1,))
            grads.x_send((1,))
        outs.x_add()
        outs.whole_send()
    attend_back(qkv, 0, out_grad, probs, scale, (8, 16))
    qkv_grads(0)
    if split:
        for grads in qkvs:
            grads.core_send((0,))
        step4(2)

    def last_norm(group, carry):
        rows = rows_of(group, quarter)
        grad = None
        for half in range(2):
            for part in range(3):
                cols = slice(384 * part, 384 * (part + 1))
                term = dot(qkv[half, rows, cols], wqkv[half, part], NT)
                grad = term if grad is None else grad + term
        values = x_rows[rows, :].astype(F32)
        back, gain_grad, shift_grad = norm_back(grad, values, gain1)
        acc_g[rows, :] += back
        sums[1, 0:1, :] += gain_grad
        sums[1, 1:2, :] += shift_grad
        return carry

    lax.fori_loop(0, QUAD // 2, last_norm, 0)
    if split:
        may(7)
        for grads in qkvs:
            grads.x_add((1,))
            grads.y_send()
        for grads in qkvs:
            grads.core_add((0,))
            grads.x_send((0,))
    lax.fori_loop(QUAD // 2, QUAD, last_norm, 0)
    store(acc_g, tokens_grad)
    if split:
        def small(src, dst, kind, device):
            return pltpu.make_async_remote_copy(
                src_ref=src,
                dst_ref=dst,
                send_sem=small_send.at[kind],
                recv_sem=small_recv.at[kind],
                device_id=device,
                device_id_type=MESH,
            )

        kept = sums.at[pl.ds(0, 2)]
        over_y = small(sums.at[pl.ds(1, 2)], sums_in.at[0], 0, place.over_y)
        over_core = small(kept, sums_in.at[1], 1, place.over_core)
        over_x = small(kept, sums_in.at[2], 2, place.over_x)
        over_z = [
            small(kept, sums_in.at[3 + k], 3 + k, device) for k, device in enumerate(place.over_z)
        ]
        over_y.start()
        outs.whole_add()
        store(outs.mine(), gout)
        step5(2)
        over_y.wait()
        sums[0] += sums_in[0, 1]
        sums[1] += sums_in[0, 0]
        over_core.start()
        may(8, 3)
        over_core.wait()
        sums[0:2] += sums_in[1]
        over_x.start()
        over_x.wait()
        sums[0:2] += sums_in[2]
        for copy in over_z:
            copy.start()
        for grads in qkvs:
            grads.x_add((0,))
            grads.y_add()
            grads.rs_send()
        for copy in over_z:
            copy.wait()
        sums[0:2] += sums_in[3] + sums_in[4] + sums_in[5]
        for grads in qkvs:
            grads.rs_add()
            grads.ag_send()
        for part, grads in enumerate(qkvs):
            grads.ag_wait()
            store_sum(grads, gqkv, part)
    stored_all()
    for gather in pieces[:3]:
        gather.sent()


def run_layer(split, *operands):
    tokens, qkv_weight = operands[1], operands[11]
    images, width = operands[0].shape[1], tokens.shape[1]
    total = images * SLOT
    half = qkv_weight.shape[2]
    vmem = pl.BlockSpec(memory_space=pltpu.VMEM)
    anywhere = pl.BlockSpec(memory_space=pl.ANY)
    shape = jax.ShapeDtypeStruct
    if split:
        grads = [
            shape((3, width // 4, half), BF16),
            shape((half // 4, width), BF16),
            shape((BLOCKS, width // 4, 512), BF16),
            shape((BLOCKS, 128, width), BF16),
        ]
    else:
        grads = [
            shape((2, 3, width, half), BF16),
            shape((2, half, width), BF16),
            shape((2 * BLOCKS, width, 512), BF16),
            shape((2 * BLOCKS, 512, width), BF16),
        ]
    return pl.pallas_call(
        functools.partial(layer_kernel, split),
        out_shape=[
            shape((total, width), BF16),
            shape((total, width), F32),
            *grads,
            shape((3, 8, width), F32),
        ],
        in_specs=[pl.BlockSpec(memory_space=pltpu.SMEM)]
        + [anywhere] * 2
        + [vmem] * 8
        + [anywhere] * 4,
        out_specs=[anywhere] * 6 + [vmem],
        scratch_shapes=[
            pltpu.VMEM((total, width), BF16),
            pltpu.VMEM((2, 3, width, half), BF16),
            pltpu.VMEM((2, half, width), BF16),
            pltpu.VMEM((2 * BLOCKS, width, 512), BF16),
            pltpu.VMEM((2 * BLOCKS, 512, width), BF16),
            pltpu.VMEM((2, 8, 512), F32),
            pltpu.VMEM((total, width), BF16),
            pltpu.VMEM((total, width), BF16),
            pltpu.VMEM((total, width), BF16),
            pltpu.VMEM((2, total, 3 * half), BF16),
            pltpu.VMEM((total, width), BF16),
            pltpu.VMEM((4 * images * SLOT, 3 * SLOT), BF16),
            pltpu.VMEM((total, width), F32),
            pltpu.VMEM((total, width), BF16),
            pltpu.VMEM((total, width), F32),
            pltpu.VMEM((total, width), F32),
            pltpu.VMEM((total, 512), BF16),
            pltpu.VMEM((total, 512), BF16),
            pltpu.VMEM((2, total // QUAD, width), BF16),
            pltpu.SemaphoreType.DMA((3 + 8 * BLOCKS,)),
            pltpu.SemaphoreType.DMA((54,)),
            pltpu.SemaphoreType.DMA((11, 4)),
            pltpu.SemaphoreType.DMA((11, 4)),
            pltpu.VMEM((2, 2, 192, 512), BF16),
            pltpu.VMEM((2, 2, 128, width), BF16),
            pltpu.VMEM((2, 192, 512), BF16),
            pltpu.VMEM((2, 128, width), BF16),
            pltpu.VMEM((192, 512), BF16),
            pltpu.VMEM((128, width), BF16),
            pltpu.VMEM((6, 48, 512), BF16),
            pltpu.VMEM((6, 32, width), BF16),
            pltpu.VMEM((10, 96, width), BF16),
            pltpu.VMEM((6, 2, 8, width), F32),
            pltpu.SemaphoreType.DMA((6, 14)),
            pltpu.SemaphoreType.DMA((6, 14)),
            pltpu.SemaphoreType.DMA((6,)),
            pltpu.SemaphoreType.DMA((6,)),
            pltpu.SemaphoreType.REGULAR((9,)),
        ],
        compiler_params=pltpu.CompilerParams(
            collective_id=0, has_side_effects=True, vmem_limit_bytes=64 * 2**20 - 2**17
        ),
    )(*operands)


def local(
    tokens,
    counts,
    norm1_gain,
    norm1_shift,
    qkv_weight,
    qv_bias,
    out_weight,
    out_bias,
    norm2_gain,
    norm2_shift,
    up_weight,
    up_bias,
    down_weight,
    down_bias,
    cotangent,
):
    images, slots, width = tokens.shape
    inner = lax.axis_size("inner")
    head_width = qkv_weight.shape[2]
    hidden = up_weight.shape[1]
    split = inner == 4 and lax.axis_size("outer") == 4
    place = lax.axis_index("inner")
    mixed, tokens_grad, gqkv, gout, gup, gdown, sums = run_layer(
        split,
        counts,
        tokens.transpose(1, 0, 2).reshape(slots * images, width),
        cotangent.transpose(1, 0, 2).reshape(slots * images, width),
        norm1_gain,
        norm1_shift,
        out_bias,
        norm2_gain,
        norm2_shift,
        down_bias,
        qv_bias,
        up_bias,
        qkv_weight.transpose(1, 0, 2),
        out_weight,
        up_weight,
        down_weight,
    )
    mixed = mixed.reshape(images, SLOT, width)[:, :slots]
    tokens_grad = tokens_grad.reshape(images, SLOT, width)[:, :slots]
    if split:
        gqkv = gqkv.transpose(1, 0, 2).astype(F32)
        gout = gout.astype(F32)
        gup = gup.reshape(BLOCKS, width // inner, 4, 128).transpose(1, 2, 0, 3)
        gup = gup.reshape(width // inner, hidden).astype(F32)
        gdown = gdown.reshape(hidden // inner, width).astype(F32)
        cut = width // inner
        shared = lax.dynamic_slice(sums[1], (0, place * cut), (6, cut))
        vectors = [shared[k] for k in range(6)]
        cut = head_width // inner
        qv_sum = lax.dynamic_slice(sums[0], (0, place * cut), (2, cut))
        up_sum = lax.dynamic_slice(sums[0], (2, place * 128), (BLOCKS, 128)).reshape(-1)
    else:

        def own_half(first, second):
            other = lax.ppermute(second.astype(BF16), "tensor", [(0, 1), (1, 0)])
            return (first.astype(F32) + other.astype(F32)).astype(BF16)

        def reduce(grads, dim=0):
            part = lax.psum_scatter(grads, "inner", scatter_dimension=dim, tiled=True)
            return lax.psum(part, "outer").astype(F32)

        gqkv = reduce(own_half(*gqkv).transpose(1, 0, 2))
        gout = reduce(own_half(*gout))
        gup = own_half(gup[:BLOCKS], gup[BLOCKS:])
        gup = gup.reshape(BLOCKS, width, 4, 128).transpose(1, 2, 0, 3).reshape(width, hidden)
        gup = reduce(gup)
        gdown = own_half(gdown[:BLOCKS], gdown[BLOCKS:])
        gdown = gdown.reshape(BLOCKS, 4, 128, width).transpose(1, 0, 2, 3)
        gdown = reduce(gdown.reshape(hidden, width))
        own = own_half(sums[0], sums[2])
        qv_sum = reduce(own[:2, :head_width].T).T
        up_sum = own[2 : 2 + BLOCKS, :512].reshape(BLOCKS, 4, 128).transpose(1, 0, 2)
        up_sum = reduce(up_sum.reshape(hidden))
        vectors = reduce(lax.psum(sums[1].astype(BF16), "tensor").T).T
    return (
        mixed,
        tokens_grad,
        vectors[0],
        vectors[1],
        gqkv,
        qv_sum,
        gout,
        vectors[2],
        vectors[3],
        vectors[4],
        gup,
        up_sum,
        gdown,
        vectors[5],
    )


def solution(mesh):
    in_specs = (
        P(("tensor", "inner", "outer"), None, None),
        P(None, ("inner", "outer")),
        P(),
        P(),
        P(None, None, "tensor"),
        P(None, "tensor"),
        P("tensor", None),
        P(),
        P(),
        P(),
        P(None, "tensor"),
        P("tensor"),
        P("tensor", None),
        P(),
        P(("tensor", "inner", "outer"), None, None),
    )
    out_specs = (
        P(("tensor", "inner", "outer"), None, None),
        P(("tensor", "inner", "outer"), None, None),
        P("inner"),
        P("inner"),
        P("inner", None, "tensor"),
        P(None, ("tensor", "inner")),
        P(("tensor", "inner"), None),
        P("inner"),
        P("inner"),
        P("inner"),
        P("inner", "tensor"),
        P(("tensor", "inner")),
        P(("tensor", "inner"), None),
        P("inner"),
    )
    return jax.shard_map(local, mesh=mesh, in_specs=in_specs, out_specs=out_specs, check_vma=False)
```

```python
import functools

import jax
import jax.numpy as jnp
from jax import lax
from jax.experimental import pallas as pl
from jax.experimental.pallas import tpu as pltpu
from jax.sharding import PartitionSpec as P

F32 = jnp.float32
BF16 = jnp.bfloat16
HEAD_DIM = 64
SLOT = 80
QUAD = 4
MESH = pl.DeviceIdType.MESH
BLOCKS = 3


def dot(left, right, dims):
    return lax.dot_general(left, right, (dims, ((), ())), preferred_element_type=F32)


NN = ((1,), (0,))
NT = ((1,), (1,))
TN = ((0,), (0,))


def rows_of(index, size):
    return pl.ds(pl.multiple_of(index * size, size), size)


def norm_stats(values):
    mean = jnp.mean(values, axis=-1, keepdims=True)
    centered = values - mean
    rstd = lax.rsqrt(jnp.mean(centered * centered, axis=-1, keepdims=True) + 1e-6)
    return centered * rstd, rstd


def norm_back(grad, values, gain):
    hat, rstd = norm_stats(values)
    scaled = grad * gain
    first = jnp.mean(scaled, axis=-1, keepdims=True)
    second = jnp.mean(scaled * hat, axis=-1, keepdims=True)
    back = rstd * (scaled - first - hat * second)
    gain_grad = jnp.sum(grad * hat, axis=0, keepdims=True)
    shift_grad = jnp.sum(grad, axis=0, keepdims=True)
    return back, gain_grad, shift_grad


def head_masks():
    head = lax.broadcasted_iota(jnp.int32, (SLOT, 256), 1) // HEAD_DIM
    return [[head == 0, head == 1, head == 2], [head == 1, head == 2, head == 3]]


def stack_heads(values, masks):
    zero = jnp.zeros_like(values)
    return jnp.concatenate([jnp.where(mask, values, zero) for mask in masks], axis=0)


def unstack_heads(values, masks):
    parts = [values[SLOT * i : SLOT * (i + 1)] for i in range(3)]
    return sum(jnp.where(mask, part, 0.0) for mask, part in zip(masks, parts))


def put_heads(ref, rows, start, first, second):
    ref[rows, start : start + 128] = first[:, :128].astype(BF16)
    ref[rows, start + 128 : start + 256] = (first[:, 128:] + second[:, :128]).astype(BF16)
    ref[rows, start + 256 : start + 384] = second[:, 128:].astype(BF16)


def attend(count_of, qkv, half, out, probs, scale, images):
    def one_image(image, carry):
        rows = rows_of(image, SLOT)
        live = lax.broadcasted_iota(jnp.int32, (SLOT, 3 * SLOT), 0) < count_of(image)
        parts = []
        for group, masks in enumerate(head_masks()):
            at = 128 * group
            query = qkv[half, rows, at : at + 256]
            key = qkv[half, rows, 384 + at : 384 + at + 256]
            value = qkv[half, rows, 768 + at : 768 + at + 256]
            scores = dot(key, stack_heads(query, masks), NT) * scale
            scores = jnp.where(live, scores, -1e9)
            top = jnp.max(scores, axis=0, keepdims=True)
            powers = jnp.exp(scores - top)
            weights = (powers / jnp.sum(powers, axis=0, keepdims=True)).astype(BF16)
            probs[rows_of((half * 16 + image) * 2 + group, SLOT), :] = weights
            parts.append(unstack_heads(dot(weights, value, TN), masks))
        put_heads(out, rows, half * 384, *parts)
        return carry

    lax.fori_loop(*images, one_image, 0, unroll=8)


def attend_back(qkv, half, out_grad, probs, scale, images):
    def one_image(image, carry):
        rows = rows_of(image, SLOT)
        queries, keys, values = [], [], []
        for group, masks in enumerate(head_masks()):
            at = 128 * group
            query = stack_heads(qkv[half, rows, at : at + 256], masks)
            key = qkv[half, rows, 384 + at : 384 + at + 256]
            value = qkv[half, rows, 768 + at : 768 + at + 256]
            grad = out_grad[rows, half * 384 + at : half * 384 + at + 256]
            grad = stack_heads(grad, masks)
            low = probs[rows_of((half * 16 + image) * 2 + group, SLOT), :]
            weights = low.astype(F32)
            prob_grad = dot(value, grad, NT)
            delta = jnp.sum(prob_grad * weights, axis=0, keepdims=True)
            score_grad = (weights * (prob_grad - delta)).astype(BF16)
            values.append(dot(low, grad, NN))
            keys.append(dot(score_grad, query, NN) * scale)
            queries.append(unstack_heads(dot(score_grad, key, TN), masks) * scale)
        put_heads(qkv.at[half], rows, 0, *queries)
        put_heads(qkv.at[half], rows, 384, *keys)
        put_heads(qkv.at[half], rows, 768, *values)
        return carry

    lax.fori_loop(*images, one_image, 0, unroll=8)


class Gather:
    def __init__(self, own, other, place, send, recv):
        self.place, self.send, self.recv = place, send, recv
        tensor, inner, outer = place.at
        whole = not place.split
        self.hop_y = self.copy(own(inner, whole), other(inner, whole), 0, place.over_y)
        self.hops = [self.hop_y]
        if place.split:
            across = lax.rem(inner + 2, 4)
            mine, theirs = other(inner, False), other(across, False)
            self.hop_x = self.copy(mine, mine, 1, place.over_x)
            self.hop_c = self.copy(mine, mine, 2, place.over_core)
            self.hop_xc = self.copy(theirs, theirs, 3, place.over_core)
            self.hops += [self.hop_x, self.hop_c, self.hop_xc]

    def copy(self, src, dst, kind, device):
        return pltpu.make_async_remote_copy(
            src_ref=src,
            dst_ref=dst,
            send_sem=self.send.at[kind],
            recv_sem=self.recv.at[kind],
            device_id=device,
            device_id_type=MESH,
        )

    def first(self):
        self.hop_y.start()

    def second(self):
        self.hop_y.wait_recv()
        if self.place.split:
            self.hop_x.start()
            self.hop_c.start()

    def third(self):
        if self.place.split:
            self.hop_x.wait_recv()
            self.hop_xc.start()

    def ready(self):
        if self.place.split:
            self.hop_c.wait_recv()
            self.hop_xc.wait_recv()

    def sent(self):
        self.hop_y.wait_send()
        self.handed_on()

    def handed_on(self):
        for hop in self.hops[1:]:
            hop.wait_send()


class Place:
    def __init__(self, split):
        self.split = split
        tensor, inner, outer = (lax.axis_index(a) for a in ("tensor", "inner", "outer"))
        self.at = (tensor, inner, outer)
        self.over_y = (1 - tensor, inner, outer)
        if split:
            core = lax.rem(inner, 2)
            self.over_x = (tensor, lax.rem(inner + 2, 4), outer)
            self.over_core = (tensor, inner + 1 - 2 * core, outer)
            self.over_z = [(tensor, inner, lax.rem(outer + step, 4)) for step in range(1, 4)]

    def meet(self):
        partners = [self.over_y]
        if self.split:
            partners += [self.over_x, self.over_core] + self.over_z
        barrier = pltpu.get_barrier_semaphore()
        for device in partners:
            pl.semaphore_signal(barrier, inc=1, device_id=device, device_id_type=MESH)
        pl.semaphore_wait(barrier, len(partners))


def add_into(target, found):
    target[...] = (target[...].astype(F32) + found[...].astype(F32)).astype(target.dtype)


class Reduce:
    CORE, X, Y, RS, AG = 0, 4, 6, 8, 11

    def __init__(self, grads, size, place, send, recv, core, first, second, outer, x_first):
        self.grads, self.size, self.place = grads, size, place
        self.send, self.recv = send, recv
        self.core, self.first, self.second, self.outer = core, first, second, outer
        self.x_first = x_first
        _, inner, self.z = place.at
        self.c, self.x = lax.rem(inner, 2), inner // 2
        self.inner = inner

    def copy(self, src, dst, kind, device):
        return pltpu.make_async_remote_copy(
            src_ref=src,
            dst_ref=dst,
            send_sem=self.send.at[kind],
            recv_sem=self.recv.at[kind],
            device_id=device,
            device_id_type=MESH,
        )

    def kept(self, half, across):
        return self.grads(half, 2 * across + self.c)

    def core_copies(self, half):
        return [
            self.copy(
                self.grads(half, 2 * across + 1 - self.c),
                self.core(half, across),
                self.CORE + 2 * half + across,
                self.place.over_core,
            )
            for across in range(2)
        ]

    def core_send(self, halves=(0, 1)):
        for half in halves:
            for copy in self.core_copies(half):
                copy.start()

    def core_add(self, halves=(0, 1)):
        for half in halves:
            for across, copy in enumerate(self.core_copies(half)):
                copy.wait()
                add_into(self.kept(half, across), self.core(half, across))

    def x_copy(self, half):
        target = self.first(half) if self.x_first else self.second()
        source = self.kept(half, 1 - self.x)
        return self.copy(source, target, self.X + half, self.place.over_x)

    def x_send(self, halves=None):
        for half in halves or ((0, 1) if self.x_first else (0,)):
            self.x_copy(half).start()

    def x_add(self, halves=None):
        for half in halves or ((0, 1) if self.x_first else (0,)):
            self.x_copy(half).wait()
            add_into(self.kept(half, self.x), self.first(half) if self.x_first else self.second())

    def y_copies(self):
        if self.x_first:
            sent = [(self.kept(1, self.x), self.second())]
        else:
            sent = [(self.kept(1, across), self.first(across)) for across in range(2)]
        return [
            self.copy(src, dst, self.Y + k, self.place.over_y) for k, (src, dst) in enumerate(sent)
        ]

    def y_send(self):
        for copy in self.y_copies():
            copy.start()

    def y_add(self):
        for across, copy in enumerate(self.y_copies()):
            copy.wait()
            if self.x_first:
                add_into(self.kept(0, self.x), self.second())
            else:
                add_into(self.kept(0, across), self.first(across))

    def mine(self):
        return self.grads(0, self.inner)

    def fourth(self, which):
        size = self.size // 4
        return self.grads(0, self.inner, pl.multiple_of(which * size, 16), size)

    def rs_copies(self):
        found = []
        for step in range(1, 4):
            there = lax.rem(self.z + step, 4)
            device = (self.place.at[0], self.inner, there)
            found.append(
                self.copy(self.fourth(there), self.outer(step - 1), self.RS + step - 1, device)
            )
        return found

    def rs_send(self):
        for copy in self.rs_copies():
            copy.start()

    def rs_add(self):
        for copy in self.rs_copies():
            copy.wait()
        total = self.fourth(self.z)[...].astype(F32)
        for step in range(3):
            total = total + self.outer(step)[...].astype(F32)
        self.fourth(self.z)[...] = total.astype(BF16)

    def ag_copies(self):
        found = []
        for step in range(1, 4):
            device = (self.place.at[0], self.inner, lax.rem(self.z + step, 4))
            part = self.fourth(self.z)
            found.append(self.copy(part, self.outer(2 + step), self.AG + step - 1, device))
        return found

    def ag_send(self):
        for copy in self.ag_copies():
            copy.start()

    def ag_wait(self):
        for copy in self.ag_copies():
            copy.wait()

    def summed(self):
        size = self.size // 4
        found = [(self.fourth(self.z), self.z * size)]
        for step in range(1, 4):
            found.append((self.outer(2 + step), lax.rem(self.z + 4 - step, 4) * size))
        return [(ref, pl.ds(pl.multiple_of(row, 16), size)) for ref, row in found]

    def whole_copies(self):
        found = []
        for step in range(1, 4):
            device = (self.place.at[0], self.inner, lax.rem(self.z + step, 4))
            found.append(self.copy(self.mine(), self.outer(step - 1), self.RS + step - 1, device))
        return found

    def whole_send(self):
        for copy in self.whole_copies():
            copy.start()

    def whole_add(self):
        for copy in self.whole_copies():
            copy.wait()
        total = self.mine()[...].astype(F32)
        for step in range(3):
            total = total + self.outer(step)[...].astype(F32)
        self.mine()[...] = total.astype(BF16)


def row_part(ref, lead, total, count, cols=None):
    def part(index, whole):
        rows = pl.ds(0, total) if whole else rows_of(index, total // count)
        return ref.at[(*lead, rows) if cols is None else (*lead, rows, cols)]

    return part


def layer_kernel(
    split,
    counts,
    tokens,
    cotangent,
    gain1_ref,
    shift1_ref,
    out_bias_ref,
    gain2_ref,
    shift2_ref,
    down_bias_ref,
    qv_bias,
    up_bias,
    qkv_weight,
    out_weight,
    up_weight,
    down_weight,
    mixed,
    tokens_grad,
    gqkv,
    gout,
    gup,
    gdown,
    sums,
    staged,
    wqkv,
    wout,
    wup,
    wdown,
    biases,
    x_rows,
    gm,
    h1,
    qkv,
    att,
    probs,
    mid,
    h2,
    acc_y,
    acc_g,
    act,
    act_grad,
    sems,
    out_sems,
    send,
    recv,
    core_up,
    core_down,
    first_up,
    first_down,
    second_up,
    second_down,
    outer_up,
    outer_down,
    out_parts,
    sums_in,
    sum_send,
    sum_recv,
    small_send,
    small_recv,
    credit,
):
    total, width = x_rows.shape
    quarter = total // QUAD
    images = counts.shape[1]
    slots = tokens.shape[0] // images
    half_width = qkv_weight.shape[2]
    scale = HEAD_DIM**-0.5
    place = Place(split)
    mine = place.at[0]

    def count_of(image):
        return counts[mine, image]

    def line(ref):
        return ref[...].reshape(1, width)

    loads = [
        pltpu.make_async_copy(tokens, staged.at[pl.ds(0, slots * images)], sems.at[0]),
        pltpu.make_async_copy(out_weight, wout.at[0], sems.at[1]),
    ]
    for part in range(3):
        loads.append(
            pltpu.make_async_copy(
                qkv_weight.at[part],
                wqkv.at[0, :, pl.ds(part * half_width, half_width)],
                sems.at[2 + part],
            )
        )
    for block in range(BLOCKS):
        for q in range(4):
            at = q * 384 + block * 128
            loads.append(
                pltpu.make_async_copy(
                    up_weight.at[:, pl.ds(at, 128)],
                    wup.at[block, :, pl.ds(q * 128, 128)],
                    sems.at[len(loads)],
                )
            )
            loads.append(
                pltpu.make_async_copy(
                    down_weight.at[pl.ds(at, 128)],
                    wdown.at[block, pl.ds(q * 128, 128)],
                    sems.at[len(loads)],
                )
            )
    for load in loads[:5]:
        load.start()
    pieces = []

    def piece(own, other):
        index = len(pieces)
        pieces.append(Gather(own, other, place, send.at[index], recv.at[index]))

    for part in range(3):
        cols = pl.ds(part * half_width, half_width)
        piece(
            row_part(qkv_weight, (part,), width, 4), row_part(wqkv, (1,), width, 4, cols)
        )
    piece(row_part(out_weight, (), half_width, 4), row_part(wout, (1,), half_width, 4))
    for block in range(BLOCKS):
        piece(row_part(wup, (block,), width, 4), row_part(wup, (BLOCKS + block,), width, 4))
        piece(row_part(wdown, (block,), 512, 4), row_part(wdown, (BLOCKS + block,), 512, 4))
    place.meet()
    for gather in pieces[:4]:
        gather.first()
    biases[0] = jnp.zeros(biases.shape[1:], F32)
    for block in range(BLOCKS):
        for q in range(4):
            at = q * 384 + block * 128
            found = up_bias[pl.ds(at, 128)].reshape(1, 128)
            biases[0, block : block + 1, q * 128 : (q + 1) * 128] = found
    biases[0, 3:4, :half_width] = qv_bias[0:1, :]
    biases[0, 3:4, 2 * half_width :] = qv_bias[1:2, :]
    bias_copy = pltpu.make_async_remote_copy(
        src_ref=biases.at[0],
        dst_ref=biases.at[1],
        send_sem=send.at[10, 0],
        recv_sem=recv.at[10, 0],
        device_id=place.over_y,
        device_id_type=MESH,
    )
    bias_copy.start()

    staged[slots * images :, :] = jnp.zeros(((SLOT - slots) * images, width), BF16)

    def by_image(target, masked):
        def some_slots(step, carry):
            values = staged[rows_of(step, 16 * images), :].astype(F32)
            values = values.reshape(16, images, width)
            values = jnp.swapaxes(values, 0, 1)
            for image in range(images):
                rows = pl.ds(pl.multiple_of(image * SLOT + step * 16, 16), 16)
                found = values[image]
                if masked:
                    slot = lax.broadcasted_iota(jnp.int32, (16, width), 0) + step * 16
                    found = jnp.where(slot < count_of(image), found, 0.0)
                target[rows, :] = found.astype(BF16)
            return carry

        lax.fori_loop(0, SLOT // 16, some_slots, 0)

    loads[0].wait()
    for load in loads[5:]:
        load.start()
    by_image(x_rows, False)
    load = pltpu.make_async_copy(cotangent, staged.at[pl.ds(0, slots * images)], sems.at[0])
    load.start()
    sums[...] = jnp.zeros_like(sums)
    gain1, shift1, gain2, shift2 = (
        line(r) for r in (gain1_ref, shift1_ref, gain2_ref, shift2_ref)
    )
    out_bias, down_bias = line(out_bias_ref), line(down_bias_ref)

    def first_norm(group, carry):
        rows = rows_of(group, quarter)
        hat, _ = norm_stats(x_rows[rows, :].astype(F32))
        h1[rows, :] = (hat * gain1 + shift1).astype(BF16)
        return carry

    lax.fori_loop(0, QUAD, first_norm, 0)
    for later in loads[1:5]:
        later.wait()
    pieces[0].second()

    def project(half, start, stop):
        cols = slice(start, stop)
        found = dot(h1[...], wqkv[half, :, cols], NN) + biases[half, 3:4, cols]
        qkv[half, :, cols] = found.astype(BF16)

    project(0, 0, 512)
    project(0, 512, 1024)
    project(0, 1024, 1152)
    pieces[1].second()
    load.wait()
    by_image(gm, True)
    pieces[2].second()
    pieces[0].third()
    for later in loads[5:]:
        later.wait()
    for gather in pieces[4:]:
        gather.first()
    attend(count_of, qkv, 0, att, probs, scale, (0, 8))
    pieces[1].third()
    attend(count_of, qkv, 0, att, probs, scale, (8, 16))
    pieces[2].third()
    pieces[3].second()
    bias_copy.wait()
    pieces[0].ready()
    pieces[1].ready()
    project(1, 0, 512)
    pieces[2].ready()
    project(1, 512, 1024)
    project(1, 1024, 1152)
    pieces[3].third()
    pieces[4].second()
    attend(count_of, qkv, 1, att, probs, scale, (0, 8))
    pieces[5].second()
    attend(count_of, qkv, 1, att, probs, scale, (8, 16))
    pieces[3].ready()
    pieces[4].third()
    pieces[6].second()

    for part in range(3):
        cols = slice(256 * part, 256 * (part + 1))
        weight = wout[:, :, cols].reshape(width, 256)
        mid[:, cols] = (
            x_rows[:, cols].astype(F32) + dot(att[...], weight, NN) + out_bias[:, cols]
        )

    pieces[5].third()

    def second_norm(group, carry):
        rows = rows_of(group, quarter)
        hat, _ = norm_stats(mid[rows, :])
        h2[rows, :] = (hat * gain2 + shift2).astype(BF16)
        sums[1, 5:6, :] += jnp.sum(gm[rows, :].astype(F32), axis=0, keepdims=True)
        return carry

    lax.fori_loop(0, QUAD, second_norm, 0)
    pieces[7].second()

    inner = place.at[1]

    def up_part(block):
        def part(half, q, start=0, size=192):
            return wup.at[half * BLOCKS + block, pl.ds(pl.multiple_of(q * 192 + start, 16), size)]

        return part

    def down_part(block):
        def part(half, q, start=0, size=128):
            return wdown.at[half * BLOCKS + block, pl.ds(pl.multiple_of(q * 128 + start, 16), size)]

        return part

    def out_part(half, q, start=0, size=96):
        return wout.at[half, pl.ds(pl.multiple_of(q * 96 + start, 16), size)]

    homes = [
        [(gm, 0), (gm, 384), (staged, 384)],
        [(att, 0), (att, 384), (staged, 0)],
    ]

    def qkv_part(which):
        def part(half, q, start=0, size=192):
            ref, col = homes[half][which]
            rows = pl.ds(pl.multiple_of(q * 192 + start, 16), size)
            return ref.at[rows, pl.ds(col, 384)]

        return part

    spare = [
        (ref, row, col) for ref in (att, gm, staged) for row in (768, 960) for col in (0, 384)
    ] + [(ref, 192 * k, 0) for ref in (act, act_grad) for k in range(6)]

    def taken(index):
        ref, row, col = spare[index]
        return ref.at[pl.ds(row, 192), pl.ds(col, 384)]

    few = [
        (ref, row, col) for ref in (att, gm, staged) for row in (1152, 1200) for col in (0, 384)
    ] + [(ref, row, 0) for ref in (act, act_grad) for row in (1152, 1200)]

    def taken_few(part, step):
        if part == 2:
            ref, row, col = act_grad, 576 + 48 * step, 0
        else:
            ref, row, col = few[6 * part + step]
        return ref.at[pl.ds(row, 48), pl.ds(col, 384)]

    ups, downs, qkvs = [], [], []
    if split:
        for block in range(BLOCKS):
            ups.append(
                Reduce(
                    up_part(block), 192, place, sum_send.at[0], sum_recv.at[0],
                    lambda half, across: core_up.at[half, across],
                    lambda across: first_up.at[across],
                    lambda: second_up,
                    lambda step: outer_up.at[step],
                    False,
                )
            )
            downs.append(
                Reduce(
                    down_part(block), 128, place, sum_send.at[1], sum_recv.at[1],
                    lambda half, across: core_down.at[half, across],
                    lambda half: first_down.at[half],
                    lambda: second_down,
                    lambda step: outer_down.at[step],
                    True,
                )
            )
        outs = Reduce(
            out_part, 96, place, sum_send.at[2], sum_recv.at[2],
            lambda half, across: out_parts.at[2 * half + across],
            lambda across: out_parts.at[4 + across],
            lambda: out_parts.at[6],
            lambda step: out_parts.at[7 + step],
            False,
        )
        for part in range(3):
            qkvs.append(
                Reduce(
                    qkv_part(part), 192, place, sum_send.at[3 + part], sum_recv.at[3 + part],
                    lambda half, across, part=part: taken(4 * part + 2 * half + across),
                    lambda half, part=part: taken(12 + 2 * part + half),
                    lambda part=part: taken(18 + part),
                    lambda step, part=part: taken_few(part, step),
                    True,
                )
            )

    def free(index, device):
        pl.semaphore_signal(credit.at[index], inc=1, device_id=device, device_id_type=MESH)

    def may(index, count=1):
        pl.semaphore_wait(credit.at[index], count)

    stores = []

    def store(src, dst):
        copy = pltpu.make_async_copy(src, dst, out_sems.at[12 + len(stores)])
        copy.start()
        stores.append(copy)

    def store_sum(grads, ref, lead):
        for part, rows in grads.summed():
            store(part, ref.at[lead, rows])

    stored = []

    def stored_all():
        for copy in stores[len(stored) :]:
            copy.wait()
            stored.append(copy)

    def step0(block):
        if block:
            may(0)
        ups[block].core_send()
        downs[block].core_send()

    def step1(block):
        ups[block].core_add()
        downs[block].core_add()
        if block < BLOCKS - 1:
            free(0, place.over_core)
        if block:
            may(1)
            may(2)
        ups[block].y_send()
        downs[block].x_send()

    def step2(block):
        ups[block].y_add()
        downs[block].x_add()
        if block < BLOCKS - 1:
            free(1, place.over_y)
            free(2, place.over_x)
        if block:
            may(3)
            may(4)
        ups[block].x_send()
        downs[block].y_send()

    def step3(block):
        ups[block].x_add()
        downs[block].y_add()
        if block < BLOCKS - 1:
            free(3, place.over_x)
            free(4, place.over_y)
        stored_all()
        ups[block].rs_send()
        downs[block].rs_send()

    def step4(block):
        ups[block].rs_add()
        downs[block].rs_add()
        ups[block].ag_send()
        downs[block].ag_send()

    def step5(block):
        ups[block].ag_wait()
        downs[block].ag_wait()
        store_sum(ups[block], gup, block)
        store_sum(downs[block], gdown, block)

    hooks = [
        [pieces[8].second, pieces[9].second, pieces[6].third, pieces[7].third],
        [pieces[8].third, pieces[9].third],
        [],
        [],
        [],
        [],
    ]
    if split:
        later = [
            (1, [(step0, 0)]),
            (2, [(step1, 0)]),
            (3, [(step2, 0), (step0, 1)]),
            (4, [(step3, 0), (step1, 1)]),
            (5, [(step4, 0), (step2, 1), (step0, 2)]),
        ]
        for order, calls in later:
            hooks[order] += [functools.partial(call, block) for call, block in calls]
    for order in range(2 * BLOCKS):
        half, block = order % 2, order // 2
        index = half * BLOCKS + block
        bias = biases[half, block : block + 1, :512]
        if half == 1:
            pieces[4 + 2 * block].ready()
            pieces[5 + 2 * block].ready()

        for part in range(2):
            cols = slice(256 * part, 256 * (part + 1))
            u = dot(h2[...], wup[index, :, cols], NN) + bias[:, cols]
            cdf = 0.5 * (1.0 + lax.erf(u * 0.7071067811865476))
            act[:, cols] = (u * cdf).astype(BF16)
            slope = cdf + u * jnp.exp(-0.5 * u * u) * 0.3989422804014327
            low = (dot(gm[...], wdown[index, cols, :], NT) * slope).astype(BF16)
            act_grad[:, cols] = low
            sums[2 * half, 2 + block : 3 + block, cols] = jnp.sum(
                low.astype(F32), axis=0, keepdims=True
            )
        for part in range(3):
            cols = slice(256 * part, 256 * (part + 1))
            y = dot(act[...], wdown[index, :, cols], NN)
            g = dot(act_grad[...], wup[index, cols, :], NT)
            if order == 0:
                acc_y[:, cols] = y
                acc_g[:, cols] = g
            else:
                acc_y[:, cols] += y
                acc_g[:, cols] += g
        if half == 1:
            pieces[4 + 2 * block].handed_on()
            pieces[5 + 2 * block].handed_on()
        gup_now = dot(h2[...], act_grad[...], TN).astype(BF16)
        gdown_now = dot(act[...], gm[...], TN).astype(BF16)
        if half == 0:
            pieces[4 + 2 * block].hop_y.wait_send()
            pieces[5 + 2 * block].hop_y.wait_send()
        wup[index] = gup_now
        wdown[index] = gdown_now
        for step in hooks[order]:
            step()

    if not split:
        store(wup, gup)
        store(wdown, gdown)

    def finish(group, carry):
        rows = rows_of(group, quarter)

        values = mid[rows, :]
        acc_y[rows, :] += values + down_bias
        back, gain_grad, shift_grad = norm_back(acc_g[rows, :], values, gain2)
        grad = gm[rows, :].astype(F32) + back
        acc_g[rows, :] = grad
        gm[rows, :] = grad.astype(BF16)
        sums[1, 2:3, :] += jnp.sum(grad, axis=0, keepdims=True)
        sums[1, 3:4, :] += gain_grad
        sums[1, 4:5, :] += shift_grad
        return carry

    lax.fori_loop(0, QUAD, finish, 0)
    if split:
        step5(0)
        step3(1)
        step1(2)

    out_grad = h2
    for part in range(3):
        cols = slice(256 * part, 256 * (part + 1))
        weight = wout[...].reshape(width, width)[cols]
        out_grad[:, cols] = dot(gm[...], weight, NT).astype(BF16)
    pieces[3].sent()
    for half in range(2):
        cols = slice(384 * half, 384 * (half + 1))
        wout[half] = dot(att[:, cols], gm[...], TN).astype(BF16)
    if split:
        outs.core_send()
        free(5, place.over_core)
        free(6, place.over_x)
        free(7, place.over_y)
        for device in place.over_z:
            free(8, device)
    else:
        store(wout, gout)

    def qkv_grads(half):
        for start, stop in ((0, 512), (512, 1024), (1024, 1152)):
            grads = qkv[half, :, start:stop]
            found = dot(h1[...], grads, TN).astype(BF16)
            for part in range(3):
                low, high = max(start, 384 * part), min(stop, 384 * (part + 1))
                if low < high:
                    home, col = homes[half][part]
                    at = col + low - 384 * part
                    home[:width, at : at + high - low] = found[:, low - start : high - start]
        for at in range(2):
            grads = qkv[half, :, 768 * at : 768 * at + 384].astype(F32)
            sums[2 * half, at : at + 1, :half_width] = jnp.sum(grads, axis=0, keepdims=True)
        if not split:
            for part, (home, col) in enumerate(homes[half]):
                store(home.at[pl.ds(0, width), pl.ds(col, 384)], gqkv.at[half, part])

    attend_back(qkv, 1, out_grad, probs, scale, (0, 8))
    if split:
        outs.core_add()
        outs.y_send()
        step4(1)
        step2(2)
    attend_back(qkv, 1, out_grad, probs, scale, (8, 16))
    qkv_grads(1)
    if split:
        may(5)
        for grads in qkvs:
            grads.core_send((1,))
        outs.y_add()
        outs.x_send()
        step5(1)
        step3(2)
    attend_back(qkv, 0, out_grad, probs, scale, (0, 8))
    if split:
        may(6)
        for grads in qkvs:
            grads.core_add((1,))
            grads.x_send((1,))
        outs.x_add()
        outs.whole_send()
    attend_back(qkv, 0, out_grad, probs, scale, (8, 16))
    qkv_grads(0)
    if split:
        for grads in qkvs:
            grads.core_send((0,))
        step4(2)

    def last_norm(group, carry):
        rows = rows_of(group, quarter)
        grad = dot(qkv[0, rows, :], wqkv[0], NT) + dot(qkv[1, rows, :], wqkv[1], NT)
        values = x_rows[rows, :].astype(F32)
        back, gain_grad, shift_grad = norm_back(grad, values, gain1)
        acc_g[rows, :] += back
        sums[1, 0:1, :] += gain_grad
        sums[1, 1:2, :] += shift_grad
        return carry

    lax.fori_loop(0, QUAD // 2, last_norm, 0)
    if split:
        may(7)
        for grads in qkvs:
            grads.x_add((1,))
            grads.y_send()
        for grads in qkvs:
            grads.core_add((0,))
            grads.x_send((0,))
    lax.fori_loop(QUAD // 2, QUAD, last_norm, 0)
    def by_slot(source, target):
        def some_slots(step, carry):
            parts = []
            for image in range(images):
                parts.append(source[pl.ds(pl.multiple_of(image * SLOT + step * 16, 16), 16), :])
            values = jnp.concatenate(parts, axis=0).reshape(images, 16, width)
            values = jnp.swapaxes(values, 0, 1).reshape(16 * images, width)
            target[rows_of(step, 16 * images), :] = values.astype(target.dtype)
            return carry

        lax.fori_loop(0, SLOT // 16, some_slots, 0)

    if split:
        def small(src, dst, kind, device):
            return pltpu.make_async_remote_copy(
                src_ref=src,
                dst_ref=dst,
                send_sem=small_send.at[kind],
                recv_sem=small_recv.at[kind],
                device_id=device,
                device_id_type=MESH,
            )

        kept = sums.at[pl.ds(0, 2)]
        over_y = small(sums.at[pl.ds(1, 2)], sums_in.at[0], 0, place.over_y)
        over_core = small(kept, sums_in.at[1], 1, place.over_core)
        over_x = small(kept, sums_in.at[2], 2, place.over_x)
        over_z = [
            small(kept, sums_in.at[3 + k], 3 + k, device) for k, device in enumerate(place.over_z)
        ]

        def qkv_rs(part):
            qkvs[part].x_add((0,))
            qkvs[part].y_add()
            qkvs[part].rs_send()

        over_y.start()
        may(8, 3)
        qkv_rs(0)
        over_y.wait()
        sums[0] += sums_in[0, 1]
        sums[1] += sums_in[0, 0]
        over_core.start()
        qkv_rs(1)
        over_core.wait()
        sums[0:2] += sums_in[1]
        over_x.start()
        qkv_rs(2)
        over_x.wait()
        sums[0:2] += sums_in[2]
        for copy in over_z:
            copy.start()
        outs.whole_add()
        store(outs.mine(), gout)
        step5(2)
        by_slot(acc_y, x_rows)
        store(x_rows.at[pl.ds(0, slots * images)], mixed)
        for grads in qkvs:
            grads.rs_add()
            grads.ag_send()
        by_slot(acc_g, acc_y)
        store(acc_y.at[pl.ds(0, slots * images)], tokens_grad)
        for copy in over_z:
            copy.wait()
        sums[0:2] += sums_in[3] + sums_in[4] + sums_in[5]
        for part, grads in enumerate(qkvs):
            grads.ag_wait()
            store_sum(grads, gqkv, part)
    else:
        by_slot(acc_y, x_rows)
        store(x_rows.at[pl.ds(0, slots * images)], mixed)
        stored_all()
        by_slot(acc_g, acc_y)
        store(acc_y.at[pl.ds(0, slots * images)], tokens_grad)
    stored_all()
    for gather in pieces[:3]:
        gather.sent()


def run_layer(split, *operands):
    tokens, qkv_weight = operands[1], operands[11]
    images, width = operands[0].shape[1], tokens.shape[1]
    total = images * SLOT
    half = qkv_weight.shape[2]
    vmem = pl.BlockSpec(memory_space=pltpu.VMEM)
    anywhere = pl.BlockSpec(memory_space=pl.ANY)
    shape = jax.ShapeDtypeStruct
    if split:
        grads = [
            shape((3, width // 4, half), BF16),
            shape((half // 4, width), BF16),
            shape((BLOCKS, width // 4, 512), BF16),
            shape((BLOCKS, 128, width), BF16),
        ]
    else:
        grads = [
            shape((2, 3, width, half), BF16),
            shape((2, half, width), BF16),
            shape((2 * BLOCKS, width, 512), BF16),
            shape((2 * BLOCKS, 512, width), BF16),
        ]
    return pl.pallas_call(
        functools.partial(layer_kernel, split),
        out_shape=[
            shape(tokens.shape, BF16),
            shape(tokens.shape, F32),
            *grads,
            shape((3, 8, width), F32),
        ],
        in_specs=[pl.BlockSpec(memory_space=pltpu.SMEM)]
        + [anywhere] * 2
        + [vmem] * 8
        + [anywhere] * 4,
        out_specs=[anywhere] * 6 + [vmem],
        scratch_shapes=[
            pltpu.VMEM((total, width), BF16),
            pltpu.VMEM((2, width, 3 * half), BF16),
            pltpu.VMEM((2, half, width), BF16),
            pltpu.VMEM((2 * BLOCKS, width, 512), BF16),
            pltpu.VMEM((2 * BLOCKS, 512, width), BF16),
            pltpu.VMEM((2, 8, 3 * half), F32),
            pltpu.VMEM((total, width), BF16),
            pltpu.VMEM((total, width), BF16),
            pltpu.VMEM((total, width), BF16),
            pltpu.VMEM((2, total, 3 * half), BF16),
            pltpu.VMEM((total, width), BF16),
            pltpu.VMEM((4 * images * SLOT, 3 * SLOT), BF16),
            pltpu.VMEM((total, width), F32),
            pltpu.VMEM((total, width), BF16),
            pltpu.VMEM((total, width), F32),
            pltpu.VMEM((total, width), F32),
            pltpu.VMEM((total, 512), BF16),
            pltpu.VMEM((total, 512), BF16),
            pltpu.SemaphoreType.DMA((5 + 8 * BLOCKS,)),
            pltpu.SemaphoreType.DMA((54,)),
            pltpu.SemaphoreType.DMA((11, 4)),
            pltpu.SemaphoreType.DMA((11, 4)),
            pltpu.VMEM((2, 2, 192, 512), BF16),
            pltpu.VMEM((2, 2, 128, width), BF16),
            pltpu.VMEM((2, 192, 512), BF16),
            pltpu.VMEM((2, 128, width), BF16),
            pltpu.VMEM((192, 512), BF16),
            pltpu.VMEM((128, width), BF16),
            pltpu.VMEM((6, 48, 512), BF16),
            pltpu.VMEM((6, 32, width), BF16),
            pltpu.VMEM((10, 96, width), BF16),
            pltpu.VMEM((6, 2, 8, width), F32),
            pltpu.SemaphoreType.DMA((6, 14)),
            pltpu.SemaphoreType.DMA((6, 14)),
            pltpu.SemaphoreType.DMA((6,)),
            pltpu.SemaphoreType.DMA((6,)),
            pltpu.SemaphoreType.REGULAR((9,)),
        ],
        compiler_params=pltpu.CompilerParams(
            collective_id=0, has_side_effects=True, vmem_limit_bytes=64 * 2**20 - 2**17
        ),
    )(*operands)


def local(
    tokens,
    counts,
    norm1_gain,
    norm1_shift,
    qkv_weight,
    qv_bias,
    out_weight,
    out_bias,
    norm2_gain,
    norm2_shift,
    up_weight,
    up_bias,
    down_weight,
    down_bias,
    cotangent,
):
    images, slots, width = tokens.shape
    inner = lax.axis_size("inner")
    head_width = qkv_weight.shape[2]
    hidden = up_weight.shape[1]
    split = inner == 4 and lax.axis_size("outer") == 4
    place = lax.axis_index("inner")
    mixed, tokens_grad, gqkv, gout, gup, gdown, sums = run_layer(
        split,
        counts,
        tokens.transpose(1, 0, 2).reshape(slots * images, width),
        cotangent.transpose(1, 0, 2).reshape(slots * images, width),
        norm1_gain,
        norm1_shift,
        out_bias,
        norm2_gain,
        norm2_shift,
        down_bias,
        qv_bias,
        up_bias,
        qkv_weight.transpose(1, 0, 2),
        out_weight,
        up_weight,
        down_weight,
    )
    mixed = mixed.reshape(slots, images, width).transpose(1, 0, 2)
    tokens_grad = tokens_grad.reshape(slots, images, width).transpose(1, 0, 2)
    if split:
        gqkv = gqkv.transpose(1, 0, 2).astype(F32)
        gout = gout.astype(F32)
        gup = gup.reshape(BLOCKS, width // inner, 4, 128).transpose(1, 2, 0, 3)
        gup = gup.reshape(width // inner, hidden).astype(F32)
        gdown = gdown.reshape(hidden // inner, width).astype(F32)
        cut = width // inner
        shared = lax.dynamic_slice(sums[1], (0, place * cut), (6, cut))
        vectors = [shared[k] for k in range(6)]
        cut = head_width // inner
        qv_sum = lax.dynamic_slice(sums[0], (0, place * cut), (2, cut))
        up_sum = lax.dynamic_slice(sums[0], (2, place * 128), (BLOCKS, 128)).reshape(-1)
    else:

        def own_half(first, second):
            other = lax.ppermute(second.astype(BF16), "tensor", [(0, 1), (1, 0)])
            return (first.astype(F32) + other.astype(F32)).astype(BF16)

        def reduce(grads, dim=0):
            part = lax.psum_scatter(grads, "inner", scatter_dimension=dim, tiled=True)
            return lax.psum(part, "outer").astype(F32)

        gqkv = reduce(own_half(*gqkv).transpose(1, 0, 2))
        gout = reduce(own_half(*gout))
        gup = own_half(gup[:BLOCKS], gup[BLOCKS:])
        gup = gup.reshape(BLOCKS, width, 4, 128).transpose(1, 2, 0, 3).reshape(width, hidden)
        gup = reduce(gup)
        gdown = own_half(gdown[:BLOCKS], gdown[BLOCKS:])
        gdown = gdown.reshape(BLOCKS, 4, 128, width).transpose(1, 0, 2, 3)
        gdown = reduce(gdown.reshape(hidden, width))
        own = own_half(sums[0], sums[2])
        qv_sum = reduce(own[:2, :head_width].T).T
        up_sum = own[2 : 2 + BLOCKS, :512].reshape(BLOCKS, 4, 128).transpose(1, 0, 2)
        up_sum = reduce(up_sum.reshape(hidden))
        vectors = reduce(lax.psum(sums[1].astype(BF16), "tensor").T).T
    return (
        mixed,
        tokens_grad,
        vectors[0],
        vectors[1],
        gqkv,
        qv_sum,
        gout,
        vectors[2],
        vectors[3],
        vectors[4],
        gup,
        up_sum,
        gdown,
        vectors[5],
    )


def solution(mesh):
    in_specs = (
        P(("tensor", "inner", "outer"), None, None),
        P(None, ("inner", "outer")),
        P(),
        P(),
        P(None, None, "tensor"),
        P(None, "tensor"),
        P("tensor", None),
        P(),
        P(),
        P(),
        P(None, "tensor"),
        P("tensor"),
        P("tensor", None),
        P(),
        P(("tensor", "inner", "outer"), None, None),
    )
    out_specs = (
        P(("tensor", "inner", "outer"), None, None),
        P(("tensor", "inner", "outer"), None, None),
        P("inner"),
        P("inner"),
        P("inner", None, "tensor"),
        P(None, ("tensor", "inner")),
        P(("tensor", "inner"), None),
        P("inner"),
        P("inner"),
        P("inner"),
        P("inner", "tensor"),
        P(("tensor", "inner")),
        P(("tensor", "inner"), None),
        P("inner"),
    )
    return jax.shard_map(local, mesh=mesh, in_specs=in_specs, out_specs=out_specs, check_vma=False)
```

```python
import functools

import jax
import jax.numpy as jnp
from jax import lax
from jax.experimental import pallas as pl
from jax.experimental.pallas import tpu as pltpu
from jax.sharding import PartitionSpec as P

F32 = jnp.float32
BF16 = jnp.bfloat16
HEAD_DIM = 64
SLOT = 80
QUAD = 4
MESH = pl.DeviceIdType.MESH
BLOCKS = 3


def dot(left, right, dims):
    return lax.dot_general(left, right, (dims, ((), ())), preferred_element_type=F32)


NN = ((1,), (0,))
NT = ((1,), (1,))
TN = ((0,), (0,))


def rows_of(index, size):
    return pl.ds(pl.multiple_of(index * size, size), size)


def norm_stats(values):
    mean = jnp.mean(values, axis=-1, keepdims=True)
    centered = values - mean
    rstd = lax.rsqrt(jnp.mean(centered * centered, axis=-1, keepdims=True) + 1e-6)
    return centered * rstd, rstd


def norm_back(grad, values, gain):
    hat, rstd = norm_stats(values)
    scaled = grad * gain
    first = jnp.mean(scaled, axis=-1, keepdims=True)
    second = jnp.mean(scaled * hat, axis=-1, keepdims=True)
    back = rstd * (scaled - first - hat * second)
    gain_grad = jnp.sum(grad * hat, axis=0, keepdims=True)
    shift_grad = jnp.sum(grad, axis=0, keepdims=True)
    return back, gain_grad, shift_grad


def head_masks():
    head = lax.broadcasted_iota(jnp.int32, (SLOT, 256), 1) // HEAD_DIM
    return [[head == 0, head == 1, head == 2], [head == 1, head == 2, head == 3]]


def stack_heads(values, masks):
    zero = jnp.zeros_like(values)
    return jnp.concatenate([jnp.where(mask, values, zero) for mask in masks], axis=0)


def unstack_heads(values, masks):
    parts = [values[SLOT * i : SLOT * (i + 1)] for i in range(3)]
    return sum(jnp.where(mask, part, 0.0) for mask, part in zip(masks, parts))


def put_heads(ref, rows, start, first, second):
    ref[rows, start : start + 128] = first[:, :128].astype(BF16)
    ref[rows, start + 128 : start + 256] = (first[:, 128:] + second[:, :128]).astype(BF16)
    ref[rows, start + 256 : start + 384] = second[:, 128:].astype(BF16)


def attend(count_of, qkv, half, out, probs, scale, images):
    def one_image(image, carry):
        rows = rows_of(image, SLOT)
        live = lax.broadcasted_iota(jnp.int32, (SLOT, 3 * SLOT), 0) < count_of(image)
        parts = []
        for group, masks in enumerate(head_masks()):
            at = 128 * group
            query = qkv[half, rows, at : at + 256]
            key = qkv[half, rows, 384 + at : 384 + at + 256]
            value = qkv[half, rows, 768 + at : 768 + at + 256]
            scores = dot(key, stack_heads(query, masks), NT) * scale
            scores = jnp.where(live, scores, -1e9)
            top = jnp.max(scores, axis=0, keepdims=True)
            powers = jnp.exp(scores - top)
            weights = (powers / jnp.sum(powers, axis=0, keepdims=True)).astype(BF16)
            probs[rows_of((half * 16 + image) * 2 + group, SLOT), :] = weights
            parts.append(unstack_heads(dot(weights, value, TN), masks))
        put_heads(out, rows, half * 384, *parts)
        return carry

    lax.fori_loop(*images, one_image, 0, unroll=8)


def attend_back(qkv, half, out_grad, probs, scale, images):
    def one_image(image, carry):
        rows = rows_of(image, SLOT)
        queries, keys, values = [], [], []
        for group, masks in enumerate(head_masks()):
            at = 128 * group
            query = stack_heads(qkv[half, rows, at : at + 256], masks)
            key = qkv[half, rows, 384 + at : 384 + at + 256]
            value = qkv[half, rows, 768 + at : 768 + at + 256]
            grad = out_grad[rows, half * 384 + at : half * 384 + at + 256]
            grad = stack_heads(grad, masks)
            low = probs[rows_of((half * 16 + image) * 2 + group, SLOT), :]
            weights = low.astype(F32)
            prob_grad = dot(value, grad, NT)
            delta = jnp.sum(prob_grad * weights, axis=0, keepdims=True)
            score_grad = (weights * (prob_grad - delta)).astype(BF16)
            values.append(dot(low, grad, NN))
            keys.append(dot(score_grad, query, NN) * scale)
            queries.append(unstack_heads(dot(score_grad, key, TN), masks) * scale)
        put_heads(qkv.at[half], rows, 0, *queries)
        put_heads(qkv.at[half], rows, 384, *keys)
        put_heads(qkv.at[half], rows, 768, *values)
        return carry

    lax.fori_loop(*images, one_image, 0, unroll=8)


class Gather:
    def __init__(self, own, other, place, send, recv):
        self.place, self.send, self.recv = place, send, recv
        tensor, inner, outer = place.at
        whole = not place.split
        self.hop_y = self.copy(own(inner, whole), other(inner, whole), 0, place.over_y)
        self.hops = [self.hop_y]
        if place.split:
            across = lax.rem(inner + 2, 4)
            mine, theirs = other(inner, False), other(across, False)
            self.hop_x = self.copy(mine, mine, 1, place.over_x)
            self.hop_c = self.copy(mine, mine, 2, place.over_core)
            self.hop_xc = self.copy(theirs, theirs, 3, place.over_core)
            self.hops += [self.hop_x, self.hop_c, self.hop_xc]

    def copy(self, src, dst, kind, device):
        return pltpu.make_async_remote_copy(
            src_ref=src,
            dst_ref=dst,
            send_sem=self.send.at[kind],
            recv_sem=self.recv.at[kind],
            device_id=device,
            device_id_type=MESH,
        )

    def first(self):
        self.hop_y.start()

    def second(self):
        self.hop_y.wait_recv()
        if self.place.split:
            self.hop_x.start()
            self.hop_c.start()

    def third(self):
        if self.place.split:
            self.hop_x.wait_recv()
            self.hop_xc.start()

    def ready(self):
        if self.place.split:
            self.hop_c.wait_recv()
            self.hop_xc.wait_recv()

    def sent(self):
        self.hop_y.wait_send()
        self.handed_on()

    def handed_on(self):
        for hop in self.hops[1:]:
            hop.wait_send()


class Place:
    def __init__(self, split):
        self.split = split
        tensor, inner, outer = (lax.axis_index(a) for a in ("tensor", "inner", "outer"))
        self.at = (tensor, inner, outer)
        self.over_y = (1 - tensor, inner, outer)
        if split:
            core = lax.rem(inner, 2)
            self.over_x = (tensor, lax.rem(inner + 2, 4), outer)
            self.over_core = (tensor, inner + 1 - 2 * core, outer)
            self.over_z = [(tensor, inner, lax.rem(outer + step, 4)) for step in range(1, 4)]

    def meet(self):
        partners = [self.over_y]
        if self.split:
            partners += [self.over_x, self.over_core] + self.over_z
        barrier = pltpu.get_barrier_semaphore()
        for device in partners:
            pl.semaphore_signal(barrier, inc=1, device_id=device, device_id_type=MESH)
        pl.semaphore_wait(barrier, len(partners))


def add_into(target, found):
    target[...] = (target[...].astype(F32) + found[...].astype(F32)).astype(target.dtype)


class Reduce:
    CORE, X, Y, RS, AG = 0, 4, 6, 8, 11

    def __init__(self, grads, size, place, send, recv, core, first, second, outer, x_first):
        self.grads, self.size, self.place = grads, size, place
        self.send, self.recv = send, recv
        self.core, self.first, self.second, self.outer = core, first, second, outer
        self.x_first = x_first
        _, inner, self.z = place.at
        self.c, self.x = lax.rem(inner, 2), inner // 2
        self.inner = inner

    def copy(self, src, dst, kind, device):
        return pltpu.make_async_remote_copy(
            src_ref=src,
            dst_ref=dst,
            send_sem=self.send.at[kind],
            recv_sem=self.recv.at[kind],
            device_id=device,
            device_id_type=MESH,
        )

    def kept(self, half, across):
        return self.grads(half, 2 * across + self.c)

    def core_copies(self, half):
        return [
            self.copy(
                self.grads(half, 2 * across + 1 - self.c),
                self.core(half, across),
                self.CORE + 2 * half + across,
                self.place.over_core,
            )
            for across in range(2)
        ]

    def core_send(self, halves=(0, 1)):
        for half in halves:
            for copy in self.core_copies(half):
                copy.start()

    def core_add(self, halves=(0, 1)):
        for half in halves:
            for across, copy in enumerate(self.core_copies(half)):
                copy.wait()
                add_into(self.kept(half, across), self.core(half, across))

    def x_copy(self, half):
        target = self.first(half) if self.x_first else self.second()
        source = self.kept(half, 1 - self.x)
        return self.copy(source, target, self.X + half, self.place.over_x)

    def x_send(self, halves=None):
        for half in halves or ((0, 1) if self.x_first else (0,)):
            self.x_copy(half).start()

    def x_add(self, halves=None):
        for half in halves or ((0, 1) if self.x_first else (0,)):
            self.x_copy(half).wait()
            add_into(self.kept(half, self.x), self.first(half) if self.x_first else self.second())

    def y_copies(self):
        if self.x_first:
            sent = [(self.kept(1, self.x), self.second())]
        else:
            sent = [(self.kept(1, across), self.first(across)) for across in range(2)]
        return [
            self.copy(src, dst, self.Y + k, self.place.over_y) for k, (src, dst) in enumerate(sent)
        ]

    def y_send(self):
        for copy in self.y_copies():
            copy.start()

    def y_add(self):
        for across, copy in enumerate(self.y_copies()):
            copy.wait()
            if self.x_first:
                add_into(self.kept(0, self.x), self.second())
            else:
                add_into(self.kept(0, across), self.first(across))

    def mine(self):
        return self.grads(0, self.inner)

    def fourth(self, which):
        size = self.size // 4
        return self.grads(0, self.inner, pl.multiple_of(which * size, 16), size)

    def rs_copies(self):
        found = []
        for step in range(1, 4):
            there = lax.rem(self.z + step, 4)
            device = (self.place.at[0], self.inner, there)
            found.append(
                self.copy(self.fourth(there), self.outer(step - 1), self.RS + step - 1, device)
            )
        return found

    def rs_send(self):
        for copy in self.rs_copies():
            copy.start()

    def rs_add(self):
        for copy in self.rs_copies():
            copy.wait()
        total = self.fourth(self.z)[...].astype(F32)
        for step in range(3):
            total = total + self.outer(step)[...].astype(F32)
        self.fourth(self.z)[...] = total.astype(BF16)

    def ag_copies(self):
        found = []
        for step in range(1, 4):
            device = (self.place.at[0], self.inner, lax.rem(self.z + step, 4))
            part = self.fourth(self.z)
            found.append(self.copy(part, self.outer(2 + step), self.AG + step - 1, device))
        return found

    def ag_send(self):
        for copy in self.ag_copies():
            copy.start()

    def ag_wait(self):
        for copy in self.ag_copies():
            copy.wait()

    def summed(self):
        size = self.size // 4
        found = [(self.fourth(self.z), self.z * size)]
        for step in range(1, 4):
            found.append((self.outer(2 + step), lax.rem(self.z + 4 - step, 4) * size))
        return [(ref, pl.ds(pl.multiple_of(row, 16), size)) for ref, row in found]

    def whole_copies(self):
        found = []
        for step in range(1, 4):
            device = (self.place.at[0], self.inner, lax.rem(self.z + step, 4))
            found.append(self.copy(self.mine(), self.outer(step - 1), self.RS + step - 1, device))
        return found

    def whole_send(self):
        for copy in self.whole_copies():
            copy.start()

    def whole_add(self):
        for copy in self.whole_copies():
            copy.wait()
        total = self.mine()[...].astype(F32)
        for step in range(3):
            total = total + self.outer(step)[...].astype(F32)
        self.mine()[...] = total.astype(BF16)


def row_part(ref, lead, total, count, cols=None):
    def part(index, whole):
        rows = pl.ds(0, total) if whole else rows_of(index, total // count)
        return ref.at[(*lead, rows) if cols is None else (*lead, rows, cols)]

    return part


def layer_kernel(
    split,
    counts,
    tokens,
    cotangent,
    gain1_ref,
    shift1_ref,
    out_bias_ref,
    gain2_ref,
    shift2_ref,
    down_bias_ref,
    qv_bias,
    up_bias,
    qkv_weight,
    out_weight,
    up_weight,
    down_weight,
    mixed,
    tokens_grad,
    gqkv,
    gout,
    gup,
    gdown,
    sums,
    staged,
    wqkv,
    wout,
    wup,
    wdown,
    biases,
    x_rows,
    gm,
    h1,
    qkv,
    att,
    probs,
    mid,
    h2,
    acc_y,
    acc_g,
    act,
    act_grad,
    sems,
    out_sems,
    send,
    recv,
    core_up,
    core_down,
    first_up,
    first_down,
    second_up,
    second_down,
    outer_up,
    outer_down,
    out_parts,
    sums_in,
    sum_send,
    sum_recv,
    small_send,
    small_recv,
    credit,
):
    total, width = x_rows.shape
    quarter = total // QUAD
    images = counts.shape[1]
    slots = tokens.shape[0] // images
    half_width = qkv_weight.shape[2]
    scale = HEAD_DIM**-0.5
    place = Place(split)
    mine = place.at[0]

    def count_of(image):
        return counts[mine, image]

    def line(ref):
        return ref[...].reshape(1, width)

    loads = [
        pltpu.make_async_copy(tokens, staged.at[pl.ds(0, slots * images)], sems.at[0]),
        pltpu.make_async_copy(out_weight, wout.at[0], sems.at[1]),
    ]
    for part in range(3):
        loads.append(
            pltpu.make_async_copy(
                qkv_weight.at[part],
                wqkv.at[0, :, pl.ds(part * half_width, half_width)],
                sems.at[2 + part],
            )
        )
    for block in range(BLOCKS):
        for q in range(4):
            at = q * 384 + block * 128
            loads.append(
                pltpu.make_async_copy(
                    up_weight.at[:, pl.ds(at, 128)],
                    wup.at[block, :, pl.ds(q * 128, 128)],
                    sems.at[len(loads)],
                )
            )
            loads.append(
                pltpu.make_async_copy(
                    down_weight.at[pl.ds(at, 128)],
                    wdown.at[block, pl.ds(q * 128, 128)],
                    sems.at[len(loads)],
                )
            )
    for load in loads[:5]:
        load.start()
    pieces = []

    def piece(own, other):
        index = len(pieces)
        pieces.append(Gather(own, other, place, send.at[index], recv.at[index]))

    for part in range(3):
        cols = pl.ds(part * half_width, half_width)
        piece(
            row_part(qkv_weight, (part,), width, 4), row_part(wqkv, (1,), width, 4, cols)
        )
    piece(row_part(out_weight, (), half_width, 4), row_part(wout, (1,), half_width, 4))
    for block in range(BLOCKS):
        piece(row_part(wup, (block,), width, 4), row_part(wup, (BLOCKS + block,), width, 4))
        piece(row_part(wdown, (block,), 512, 4), row_part(wdown, (BLOCKS + block,), 512, 4))
    place.meet()
    for gather in pieces[:4]:
        gather.first()
    biases[0] = jnp.zeros(biases.shape[1:], F32)
    for block in range(BLOCKS):
        for q in range(4):
            at = q * 384 + block * 128
            found = up_bias[pl.ds(at, 128)].reshape(1, 128)
            biases[0, block : block + 1, q * 128 : (q + 1) * 128] = found
    biases[0, 3:4, :half_width] = qv_bias[0:1, :]
    biases[0, 3:4, 2 * half_width :] = qv_bias[1:2, :]
    bias_copy = pltpu.make_async_remote_copy(
        src_ref=biases.at[0],
        dst_ref=biases.at[1],
        send_sem=send.at[10, 0],
        recv_sem=recv.at[10, 0],
        device_id=place.over_y,
        device_id_type=MESH,
    )
    bias_copy.start()

    staged[slots * images :, :] = jnp.zeros(((SLOT - slots) * images, width), BF16)

    def by_image(target, masked):
        def some_slots(step, carry):
            values = staged[rows_of(step, 16 * images), :].astype(F32)
            values = values.reshape(16, images, width)
            values = jnp.swapaxes(values, 0, 1)
            for image in range(images):
                rows = pl.ds(pl.multiple_of(image * SLOT + step * 16, 16), 16)
                found = values[image]
                if masked:
                    slot = lax.broadcasted_iota(jnp.int32, (16, width), 0) + step * 16
                    found = jnp.where(slot < count_of(image), found, 0.0)
                target[rows, :] = found.astype(BF16)
            return carry

        lax.fori_loop(0, SLOT // 16, some_slots, 0)

    loads[0].wait()
    for load in loads[5:]:
        load.start()
    by_image(x_rows, False)
    load = pltpu.make_async_copy(cotangent, staged.at[pl.ds(0, slots * images)], sems.at[0])
    load.start()
    sums[...] = jnp.zeros_like(sums)
    gain1, shift1, gain2, shift2 = (
        line(r) for r in (gain1_ref, shift1_ref, gain2_ref, shift2_ref)
    )
    out_bias, down_bias = line(out_bias_ref), line(down_bias_ref)

    def first_norm(group, carry):
        rows = rows_of(group, quarter)
        hat, _ = norm_stats(x_rows[rows, :].astype(F32))
        h1[rows, :] = (hat * gain1 + shift1).astype(BF16)
        return carry

    lax.fori_loop(0, QUAD, first_norm, 0)
    for later in loads[1:5]:
        later.wait()
    pieces[0].second()

    def project(half, start, stop):
        cols = slice(start, stop)
        found = dot(h1[...], wqkv[half, :, cols], NN) + biases[half, 3:4, cols]
        qkv[half, :, cols] = found.astype(BF16)

    project(0, 0, 512)
    project(0, 512, 1024)
    project(0, 1024, 1152)
    pieces[1].second()
    load.wait()
    by_image(gm, True)
    pieces[2].second()
    pieces[0].third()
    for later in loads[5:]:
        later.wait()
    for gather in pieces[4:]:
        gather.first()
    attend(count_of, qkv, 0, att, probs, scale, (0, 8))
    pieces[1].third()
    attend(count_of, qkv, 0, att, probs, scale, (8, 16))
    pieces[2].third()
    pieces[3].second()
    bias_copy.wait()
    pieces[0].ready()
    pieces[1].ready()
    project(1, 0, 512)
    pieces[2].ready()
    project(1, 512, 1024)
    project(1, 1024, 1152)
    pieces[3].third()
    pieces[4].second()
    attend(count_of, qkv, 1, att, probs, scale, (0, 8))
    pieces[5].second()
    attend(count_of, qkv, 1, att, probs, scale, (8, 16))
    pieces[3].ready()
    pieces[4].third()
    pieces[6].second()

    for part in range(3):
        cols = slice(256 * part, 256 * (part + 1))
        weight = wout[:, :, cols].reshape(width, 256)
        mid[:, cols] = (
            x_rows[:, cols].astype(F32) + dot(att[...], weight, NN) + out_bias[:, cols]
        )

    pieces[5].third()

    def second_norm(group, carry):
        rows = rows_of(group, quarter)
        hat, _ = norm_stats(mid[rows, :])
        h2[rows, :] = (hat * gain2 + shift2).astype(BF16)
        sums[1, 5:6, :] += jnp.sum(gm[rows, :].astype(F32), axis=0, keepdims=True)
        return carry

    lax.fori_loop(0, QUAD, second_norm, 0)
    pieces[7].second()

    inner = place.at[1]

    def up_part(block):
        def part(half, q, start=0, size=192):
            return wup.at[half * BLOCKS + block, pl.ds(pl.multiple_of(q * 192 + start, 16), size)]

        return part

    def down_part(block):
        def part(half, q, start=0, size=128):
            return wdown.at[half * BLOCKS + block, pl.ds(pl.multiple_of(q * 128 + start, 16), size)]

        return part

    def out_part(half, q, start=0, size=96):
        return wout.at[half, pl.ds(pl.multiple_of(q * 96 + start, 16), size)]

    homes = [
        [(gm, 0), (gm, 384), (staged, 384)],
        [(att, 0), (att, 384), (staged, 0)],
    ]

    def qkv_part(which):
        def part(half, q, start=0, size=192):
            ref, col = homes[half][which]
            rows = pl.ds(pl.multiple_of(q * 192 + start, 16), size)
            return ref.at[rows, pl.ds(col, 384)]

        return part

    spare = [
        (ref, row, col) for ref in (att, gm, staged) for row in (768, 960) for col in (0, 384)
    ] + [(ref, 192 * k, 0) for ref in (act, act_grad) for k in range(6)]

    def taken(index):
        ref, row, col = spare[index]
        return ref.at[pl.ds(row, 192), pl.ds(col, 384)]

    few = [
        (ref, row, col) for ref in (att, gm, staged) for row in (1152, 1200) for col in (0, 384)
    ] + [(ref, row, 0) for ref in (act, act_grad) for row in (1152, 1200)]

    def taken_few(part, step):
        if part == 2:
            ref, row, col = act_grad, 576 + 48 * step, 0
        else:
            ref, row, col = few[6 * part + step]
        return ref.at[pl.ds(row, 48), pl.ds(col, 384)]

    ups, downs, qkvs = [], [], []
    if split:
        for block in range(BLOCKS):
            ups.append(
                Reduce(
                    up_part(block), 192, place, sum_send.at[0], sum_recv.at[0],
                    lambda half, across: core_up.at[half, across],
                    lambda across: first_up.at[across],
                    lambda: second_up,
                    lambda step: outer_up.at[step],
                    False,
                )
            )
            downs.append(
                Reduce(
                    down_part(block), 128, place, sum_send.at[1], sum_recv.at[1],
                    lambda half, across: core_down.at[half, across],
                    lambda half: first_down.at[half],
                    lambda: second_down,
                    lambda step: outer_down.at[step],
                    True,
                )
            )
        outs = Reduce(
            out_part, 96, place, sum_send.at[2], sum_recv.at[2],
            lambda half, across: out_parts.at[2 * half + across],
            lambda across: out_parts.at[4 + across],
            lambda: out_parts.at[6],
            lambda step: out_parts.at[7 + step],
            False,
        )
        for part in range(3):
            qkvs.append(
                Reduce(
                    qkv_part(part), 192, place, sum_send.at[3 + part], sum_recv.at[3 + part],
                    lambda half, across, part=part: taken(4 * part + 2 * half + across),
                    lambda half, part=part: taken(12 + 2 * part + half),
                    lambda part=part: taken(18 + part),
                    lambda step, part=part: taken_few(part, step),
                    True,
                )
            )

    def free(index, device):
        pl.semaphore_signal(credit.at[index], inc=1, device_id=device, device_id_type=MESH)

    def may(index, count=1):
        pl.semaphore_wait(credit.at[index], count)

    stores = []

    def store(src, dst):
        copy = pltpu.make_async_copy(src, dst, out_sems.at[12 + len(stores)])
        copy.start()
        stores.append(copy)

    def store_sum(grads, ref, lead):
        for part, rows in grads.summed():
            store(part, ref.at[lead, rows])

    stored = []

    def stored_all():
        for copy in stores[len(stored) :]:
            copy.wait()
            stored.append(copy)

    def step0(block):
        if block:
            may(0)
        ups[block].core_send()
        downs[block].core_send()

    def step1(block):
        ups[block].core_add()
        downs[block].core_add()
        if block < BLOCKS - 1:
            free(0, place.over_core)
        if block:
            may(1)
            may(2)
        ups[block].y_send()
        downs[block].x_send()

    def step2(block):
        ups[block].y_add()
        downs[block].x_add()
        if block < BLOCKS - 1:
            free(1, place.over_y)
            free(2, place.over_x)
        if block:
            may(3)
            may(4)
        ups[block].x_send()
        downs[block].y_send()

    def step3(block):
        ups[block].x_add()
        downs[block].y_add()
        if block < BLOCKS - 1:
            free(3, place.over_x)
            free(4, place.over_y)
        stored_all()
        ups[block].rs_send()
        downs[block].rs_send()

    def step4(block):
        ups[block].rs_add()
        downs[block].rs_add()
        ups[block].ag_send()
        downs[block].ag_send()

    def step5(block):
        ups[block].ag_wait()
        downs[block].ag_wait()
        store_sum(ups[block], gup, block)
        store_sum(downs[block], gdown, block)

    hooks = [
        [pieces[8].second, pieces[9].second, pieces[6].third, pieces[7].third],
        [pieces[8].third, pieces[9].third],
        [],
        [],
        [],
        [],
    ]
    if split:
        later = [
            (1, [(step0, 0)]),
            (2, [(step1, 0)]),
            (3, [(step2, 0), (step0, 1)]),
            (4, [(step3, 0), (step1, 1)]),
            (5, [(step4, 0), (step2, 1), (step0, 2)]),
        ]
        for order, calls in later:
            hooks[order] += [functools.partial(call, block) for call, block in calls]
    for order in range(2 * BLOCKS):
        half, block = order % 2, order // 2
        index = half * BLOCKS + block
        bias = biases[half, block : block + 1, :512]
        if half == 1:
            pieces[4 + 2 * block].ready()
            pieces[5 + 2 * block].ready()

        for part in range(2):
            cols = slice(256 * part, 256 * (part + 1))
            u = dot(h2[...], wup[index, :, cols], NN) + bias[:, cols]
            cdf = 0.5 * (1.0 + lax.erf(u * 0.7071067811865476))
            act[:, cols] = (u * cdf).astype(BF16)
            slope = cdf + u * jnp.exp(-0.5 * u * u) * 0.3989422804014327
            low = (dot(gm[...], wdown[index, cols, :], NT) * slope).astype(BF16)
            act_grad[:, cols] = low
            sums[2 * half, 2 + block : 3 + block, cols] = jnp.sum(
                low.astype(F32), axis=0, keepdims=True
            )
        for part in range(3):
            cols = slice(256 * part, 256 * (part + 1))
            y = dot(act[...], wdown[index, :, cols], NN)
            g = dot(act_grad[...], wup[index, cols, :], NT)
            if order == 0:
                acc_y[:, cols] = y
                acc_g[:, cols] = g
            else:
                acc_y[:, cols] += y
                acc_g[:, cols] += g
        if half == 1:
            pieces[4 + 2 * block].handed_on()
            pieces[5 + 2 * block].handed_on()
        gup_now = dot(h2[...], act_grad[...], TN).astype(BF16)
        gdown_now = dot(act[...], gm[...], TN).astype(BF16)
        if half == 0:
            pieces[4 + 2 * block].hop_y.wait_send()
            pieces[5 + 2 * block].hop_y.wait_send()
        wup[index] = gup_now
        wdown[index] = gdown_now
        for step in hooks[order]:
            step()

    if not split:
        store(wup, gup)
        store(wdown, gdown)

    def finish(group, carry):
        rows = rows_of(group, quarter)

        values = mid[rows, :]
        acc_y[rows, :] += values + down_bias
        back, gain_grad, shift_grad = norm_back(acc_g[rows, :], values, gain2)
        grad = gm[rows, :].astype(F32) + back
        acc_g[rows, :] = grad
        gm[rows, :] = grad.astype(BF16)
        sums[1, 2:3, :] += jnp.sum(grad, axis=0, keepdims=True)
        sums[1, 3:4, :] += gain_grad
        sums[1, 4:5, :] += shift_grad
        return carry

    lax.fori_loop(0, QUAD, finish, 0)
    if split:
        step5(0)
        step3(1)
        step1(2)

    out_grad = h2
    for part in range(3):
        cols = slice(256 * part, 256 * (part + 1))
        weight = wout[...].reshape(width, width)[cols]
        out_grad[:, cols] = dot(gm[...], weight, NT).astype(BF16)
    pieces[3].sent()
    for half in range(2):
        cols = slice(384 * half, 384 * (half + 1))
        wout[half] = dot(att[:, cols], gm[...], TN).astype(BF16)
    if split:
        outs.core_send()
        free(5, place.over_core)
        free(6, place.over_x)
        free(7, place.over_y)
        for device in place.over_z:
            free(8, device)
    else:
        store(wout, gout)

    def qkv_grads(half):
        for start, stop in ((0, 512), (512, 1024), (1024, 1152)):
            grads = qkv[half, :, start:stop]
            found = dot(h1[...], grads, TN).astype(BF16)
            for part in range(3):
                low, high = max(start, 384 * part), min(stop, 384 * (part + 1))
                if low < high:
                    home, col = homes[half][part]
                    at = col + low - 384 * part
                    home[:width, at : at + high - low] = found[:, low - start : high - start]
        for at in range(2):
            grads = qkv[half, :, 768 * at : 768 * at + 384].astype(F32)
            sums[2 * half, at : at + 1, :half_width] = jnp.sum(grads, axis=0, keepdims=True)
        if not split:
            for part, (home, col) in enumerate(homes[half]):
                store(home.at[pl.ds(0, width), pl.ds(col, 384)], gqkv.at[half, part])

    attend_back(qkv, 1, out_grad, probs, scale, (0, 8))
    if split:
        outs.core_add()
        outs.y_send()
        step4(1)
        step2(2)
    attend_back(qkv, 1, out_grad, probs, scale, (8, 16))
    qkv_grads(1)
    if split:
        may(5)
        for grads in qkvs:
            grads.core_send((1,))
        outs.y_add()
        outs.x_send()
        step5(1)
        step3(2)
    attend_back(qkv, 0, out_grad, probs, scale, (0, 8))
    if split:
        may(6)
        for grads in qkvs:
            grads.core_add((1,))
            grads.x_send((1,))
        outs.x_add()
        outs.whole_send()
    attend_back(qkv, 0, out_grad, probs, scale, (8, 16))
    qkv_grads(0)
    if split:
        for grads in qkvs:
            grads.core_send((0,))
        step4(2)

    def last_norm(group, carry):
        rows = rows_of(group, quarter)
        grad = dot(qkv[0, rows, :], wqkv[0], NT) + dot(qkv[1, rows, :], wqkv[1], NT)
        values = x_rows[rows, :].astype(F32)
        back, gain_grad, shift_grad = norm_back(grad, values, gain1)
        acc_g[rows, :] += back
        sums[1, 0:1, :] += gain_grad
        sums[1, 1:2, :] += shift_grad
        return carry

    lax.fori_loop(0, QUAD // 2, last_norm, 0)
    if split:
        may(7)
        for grads in qkvs:
            grads.x_add((1,))
            grads.y_send()
        for grads in qkvs:
            grads.core_add((0,))
            grads.x_send((0,))
    lax.fori_loop(QUAD // 2, QUAD, last_norm, 0)
    def by_slot(source, target):
        def some_slots(step, carry):
            parts = []
            for image in range(images):
                parts.append(source[pl.ds(pl.multiple_of(image * SLOT + step * 16, 16), 16), :])
            values = jnp.concatenate(parts, axis=0).reshape(images, 16, width)
            values = jnp.swapaxes(values, 0, 1).reshape(16 * images, width)
            target[rows_of(step, 16 * images), :] = values.astype(target.dtype)
            return carry

        lax.fori_loop(0, SLOT // 16, some_slots, 0)

    if split:
        def small(src, dst, kind, device):
            return pltpu.make_async_remote_copy(
                src_ref=src,
                dst_ref=dst,
                send_sem=small_send.at[kind],
                recv_sem=small_recv.at[kind],
                device_id=device,
                device_id_type=MESH,
            )

        kept = sums.at[pl.ds(0, 2)]
        over_y = small(sums.at[pl.ds(1, 2)], sums_in.at[0], 0, place.over_y)
        over_core = small(kept, sums_in.at[1], 1, place.over_core)
        over_x = small(kept, sums_in.at[2], 2, place.over_x)
        over_z = [
            small(kept, sums_in.at[3 + k], 3 + k, device) for k, device in enumerate(place.over_z)
        ]

        def qkv_rs(part):
            qkvs[part].x_add((0,))
            qkvs[part].y_add()
            qkvs[part].rs_send()

        over_y.start()
        may(8, 3)
        qkv_rs(0)
        over_y.wait()
        sums[0] += sums_in[0, 1]
        sums[1] += sums_in[0, 0]
        over_core.start()
        qkv_rs(1)
        over_core.wait()
        sums[0:2] += sums_in[1]
        over_x.start()
        qkv_rs(2)
        over_x.wait()
        sums[0:2] += sums_in[2]
        for copy in over_z:
            copy.start()
        outs.whole_add()
        store(outs.mine(), gout)
        step5(2)
        by_slot(acc_y, x_rows)
        store(x_rows.at[pl.ds(0, slots * images)], mixed)
        for grads in qkvs:
            grads.rs_add()
            grads.ag_send()
        by_slot(acc_g, acc_y)
        store(acc_y.at[pl.ds(0, slots * images)], tokens_grad)
        for copy in over_z:
            copy.wait()
        sums[0:2] += sums_in[3] + sums_in[4] + sums_in[5]
        for part, grads in enumerate(qkvs):
            grads.ag_wait()
            store_sum(grads, gqkv, part)
    else:
        by_slot(acc_y, x_rows)
        store(x_rows.at[pl.ds(0, slots * images)], mixed)
        stored_all()
        by_slot(acc_g, acc_y)
        store(acc_y.at[pl.ds(0, slots * images)], tokens_grad)
    stored_all()
    for gather in pieces[:3]:
        gather.sent()


def run_layer(split, *operands):
    tokens, qkv_weight = operands[1], operands[11]
    images, width = operands[0].shape[1], tokens.shape[1]
    total = images * SLOT
    half = qkv_weight.shape[2]
    vmem = pl.BlockSpec(memory_space=pltpu.VMEM)
    anywhere = pl.BlockSpec(memory_space=pl.ANY)
    shape = jax.ShapeDtypeStruct
    if split:
        grads = [
            shape((3, width // 4, half), BF16),
            shape((half // 4, width), BF16),
            shape((BLOCKS, width // 4, 512), BF16),
            shape((BLOCKS, 128, width), BF16),
        ]
    else:
        grads = [
            shape((2, 3, width, half), BF16),
            shape((2, half, width), BF16),
            shape((2 * BLOCKS, width, 512), BF16),
            shape((2 * BLOCKS, 512, width), BF16),
        ]
    return pl.pallas_call(
        functools.partial(layer_kernel, split),
        out_shape=[
            shape(tokens.shape, BF16),
            shape(tokens.shape, F32),
            *grads,
            shape((3, 8, width), F32),
        ],
        in_specs=[pl.BlockSpec(memory_space=pltpu.SMEM)]
        + [anywhere] * 2
        + [vmem] * 8
        + [anywhere] * 4,
        out_specs=[anywhere] * 6 + [vmem],
        scratch_shapes=[
            pltpu.VMEM((total, width), BF16),
            pltpu.VMEM((2, width, 3 * half), BF16),
            pltpu.VMEM((2, half, width), BF16),
            pltpu.VMEM((2 * BLOCKS, width, 512), BF16),
            pltpu.VMEM((2 * BLOCKS, 512, width), BF16),
            pltpu.VMEM((2, 8, 3 * half), F32),
            pltpu.VMEM((total, width), BF16),
            pltpu.VMEM((total, width), BF16),
            pltpu.VMEM((total, width), BF16),
            pltpu.VMEM((2, total, 3 * half), BF16),
            pltpu.VMEM((total, width), BF16),
            pltpu.VMEM((4 * images * SLOT, 3 * SLOT), BF16),
            pltpu.VMEM((total, width), F32),
            pltpu.VMEM((total, width), BF16),
            pltpu.VMEM((total, width), F32),
            pltpu.VMEM((total, width), F32),
            pltpu.VMEM((total, 512), BF16),
            pltpu.VMEM((total, 512), BF16),
            pltpu.SemaphoreType.DMA((5 + 8 * BLOCKS,)),
            pltpu.SemaphoreType.DMA((54,)),
            pltpu.SemaphoreType.DMA((11, 4)),
            pltpu.SemaphoreType.DMA((11, 4)),
            pltpu.VMEM((2, 2, 192, 512), BF16),
            pltpu.VMEM((2, 2, 128, width), BF16),
            pltpu.VMEM((2, 192, 512), BF16),
            pltpu.VMEM((2, 128, width), BF16),
            pltpu.VMEM((192, 512), BF16),
            pltpu.VMEM((128, width), BF16),
            pltpu.VMEM((6, 48, 512), BF16),
            pltpu.VMEM((6, 32, width), BF16),
            pltpu.VMEM((10, 96, width), BF16),
            pltpu.VMEM((6, 2, 8, width), F32),
            pltpu.SemaphoreType.DMA((6, 14)),
            pltpu.SemaphoreType.DMA((6, 14)),
            pltpu.SemaphoreType.DMA((6,)),
            pltpu.SemaphoreType.DMA((6,)),
            pltpu.SemaphoreType.REGULAR((9,)),
        ],
        compiler_params=pltpu.CompilerParams(
            collective_id=0, has_side_effects=True, vmem_limit_bytes=64 * 2**20 - 2**17
        ),
    )(*operands)


def widen_kernel(
    mixed,
    tokens_grad,
    gqkv,
    gout,
    gup,
    gdown,
    mixed_out,
    tokens_out,
    fqkv,
    fout,
    fup,
    fdown,
    held_mixed,
    held_tokens,
    sems,
):
    loads, stores = [], []
    ways = ((mixed, held_mixed, mixed_out), (tokens_grad, held_tokens, tokens_out))
    for source, held, target in ways:
        size = source.shape[0] // 3
        for part in range(3):
            rows = pl.ds(part * size, size)
            at = len(loads)
            loads.append(pltpu.make_async_copy(source.at[rows], held.at[rows], sems.at[at]))
            stores.append(pltpu.make_async_copy(held.at[rows], target.at[rows], sems.at[6 + at]))
            loads[-1].start()
    fqkv[...] = gqkv[...].astype(F32)
    fout[...] = gout[...].astype(F32)
    for load, store in zip(loads, stores):
        load.wait()
        store.start()
    fdown[...] = gdown[...].astype(F32)
    for block in range(BLOCKS):
        for q in range(4):
            at = q * 384 + block * 128
            fup[:, at : at + 128] = gup[block, :, q * 128 : (q + 1) * 128].astype(F32)
    for store in stores:
        store.wait()


def widen(mixed, tokens_grad, gqkv, gout, gup, gdown):
    vmem = pl.BlockSpec(memory_space=pltpu.VMEM)
    anywhere = pl.BlockSpec(memory_space=pl.ANY)
    shape = jax.ShapeDtypeStruct
    return pl.pallas_call(
        widen_kernel,
        out_shape=[
            shape(mixed.shape, BF16),
            shape(tokens_grad.shape, F32),
            shape(gqkv.shape, F32),
            shape(gout.shape, F32),
            shape((gup.shape[1], BLOCKS * gup.shape[2]), F32),
            shape(gdown.shape, F32),
        ],
        in_specs=[anywhere] * 2 + [vmem] * 4,
        out_specs=[anywhere] * 2 + [vmem] * 4,
        scratch_shapes=[
            pltpu.VMEM(mixed.shape, BF16),
            pltpu.VMEM(tokens_grad.shape, F32),
            pltpu.SemaphoreType.DMA((12,)),
        ],
        compiler_params=pltpu.CompilerParams(vmem_limit_bytes=64 * 2**20 - 2**17),
    )(mixed, tokens_grad, gqkv, gout, gup, gdown)


def local(
    tokens,
    counts,
    norm1_gain,
    norm1_shift,
    qkv_weight,
    qv_bias,
    out_weight,
    out_bias,
    norm2_gain,
    norm2_shift,
    up_weight,
    up_bias,
    down_weight,
    down_bias,
    cotangent,
):
    images, slots, width = tokens.shape
    inner = lax.axis_size("inner")
    head_width = qkv_weight.shape[2]
    hidden = up_weight.shape[1]
    split = inner == 4 and lax.axis_size("outer") == 4
    place = lax.axis_index("inner")
    mixed, tokens_grad, gqkv, gout, gup, gdown, sums = run_layer(
        split,
        counts,
        tokens.transpose(1, 0, 2).reshape(slots * images, width),
        cotangent.transpose(1, 0, 2).reshape(slots * images, width),
        norm1_gain,
        norm1_shift,
        out_bias,
        norm2_gain,
        norm2_shift,
        down_bias,
        qv_bias,
        up_bias,
        qkv_weight.transpose(1, 0, 2),
        out_weight,
        up_weight,
        down_weight,
    )
    if split:
        mixed, tokens_grad, gqkv, gout, gup, gdown = widen(
            mixed, tokens_grad, gqkv, gout, gup, gdown
        )
    mixed = mixed.reshape(slots, images, width).transpose(1, 0, 2)
    tokens_grad = tokens_grad.reshape(slots, images, width).transpose(1, 0, 2)
    if split:
        gqkv = gqkv.transpose(1, 0, 2)
        gdown = gdown.reshape(hidden // inner, width)
        cut = width // inner
        shared = lax.dynamic_slice(sums[1], (0, place * cut), (6, cut))
        vectors = [shared[k] for k in range(6)]
        cut = head_width // inner
        qv_sum = lax.dynamic_slice(sums[0], (0, place * cut), (2, cut))
        up_sum = lax.dynamic_slice(sums[0], (2, place * 128), (BLOCKS, 128)).reshape(-1)
    else:

        def own_half(first, second):
            other = lax.ppermute(second.astype(BF16), "tensor", [(0, 1), (1, 0)])
            return (first.astype(F32) + other.astype(F32)).astype(BF16)

        def reduce(grads, dim=0):
            part = lax.psum_scatter(grads, "inner", scatter_dimension=dim, tiled=True)
            return lax.psum(part, "outer").astype(F32)

        gqkv = reduce(own_half(*gqkv).transpose(1, 0, 2))
        gout = reduce(own_half(*gout))
        gup = own_half(gup[:BLOCKS], gup[BLOCKS:])
        gup = gup.reshape(BLOCKS, width, 4, 128).transpose(1, 2, 0, 3).reshape(width, hidden)
        gup = reduce(gup)
        gdown = own_half(gdown[:BLOCKS], gdown[BLOCKS:])
        gdown = gdown.reshape(BLOCKS, 4, 128, width).transpose(1, 0, 2, 3)
        gdown = reduce(gdown.reshape(hidden, width))
        own = own_half(sums[0], sums[2])
        qv_sum = reduce(own[:2, :head_width].T).T
        up_sum = own[2 : 2 + BLOCKS, :512].reshape(BLOCKS, 4, 128).transpose(1, 0, 2)
        up_sum = reduce(up_sum.reshape(hidden))
        vectors = reduce(lax.psum(sums[1].astype(BF16), "tensor").T).T
    return (
        mixed,
        tokens_grad,
        vectors[0],
        vectors[1],
        gqkv,
        qv_sum,
        gout,
        vectors[2],
        vectors[3],
        vectors[4],
        gup,
        up_sum,
        gdown,
        vectors[5],
    )


def solution(mesh):
    in_specs = (
        P(("tensor", "inner", "outer"), None, None),
        P(None, ("inner", "outer")),
        P(),
        P(),
        P(None, None, "tensor"),
        P(None, "tensor"),
        P("tensor", None),
        P(),
        P(),
        P(),
        P(None, "tensor"),
        P("tensor"),
        P("tensor", None),
        P(),
        P(("tensor", "inner", "outer"), None, None),
    )
    out_specs = (
        P(("tensor", "inner", "outer"), None, None),
        P(("tensor", "inner", "outer"), None, None),
        P("inner"),
        P("inner"),
        P("inner", None, "tensor"),
        P(None, ("tensor", "inner")),
        P(("tensor", "inner"), None),
        P("inner"),
        P("inner"),
        P("inner"),
        P("inner", "tensor"),
        P(("tensor", "inner")),
        P(("tensor", "inner"), None),
        P("inner"),
    )
    return jax.shard_map(local, mesh=mesh, in_specs=in_specs, out_specs=out_specs, check_vma=False)
```
